256 devices in a mesh: tm: 16 (over z_hi, y, core), space: 16 (over x, z_lo).
Axes of the slice: x: 4, y: 4, z: 8 (z_hi: 2, z_lo: 4; z = z_hi * 4 + z_lo), core: 2. Of those that a mesh axis runs over, the one named last changes fastest.
Arguments:
- initial: float32 [64, 4096], P(None, 'space'), may hold values from -6 to 6
- guess: float32 [16, 64, 4096], P('tm', None, 'space'), may hold values from -6 to 6
- forcing: float32 [64, 64, 4096], P('tm', None, 'space'), may hold values from -1.8 to 1.8
- fine_inverse: float32 [64, 64, 4096], P(None, None, 'space'), as said below
- coarse_inverse: float32 [64, 64, 4096], P(None, None, 'space'), as said below
- neighbour: int32 [6, 4096], P(None, 'space'), may hold values from 0 to 511, as said below
- send_low: int32 [2048], P('space'), may hold values from 0 to 255, as said below
- send_high: int32 [2048], P('space'), may hold values from 0 to 255, as said below
- trace_map: float32 [6, 32, 64], replicated, may hold values from -0.75 to 0.75
- lift_map: float32 [6, 64, 32], replicated, may hold values from -0.09 to 0.09
Outputs:
- solution: float32 [64, 64, 4096], P('tm', None, 'space')
The draws below stay inside these ranges and needn't reach their ends.
Inputs may be any that keep to these rules, and one draw needn't show every extreme that they name: `neighbour`: each block's elements form 2 x 8 x 16 hexahedra, periodic along y and z inside the block, numbered in a random order. Along x, an element's face to another block names slot 256 + k or 384 + k, where k is the face's position in the neighbouring block's boundary map; every other face names a local id. `send_low`: each block's 128 entries are its elements of the lowest x layer, face k of block s meeting face k of block s - 1's upper map. `send_high`: each block's 128 entries are its elements of the highest x layer, face k of block s meeting face k of block s + 1's lower map. `fine_inverse`: each block is a dominant diagonal plus a skew-symmetric full part. `coarse_inverse`: each block is a dominant diagonal plus a skew-symmetric full part.
All inputs are finite; a program needn't handle non-finite values.
Results may differ from the reference program's by a relative error of at most 0.00014.
Values sent between devices are 32-bit elements; how exact they have to be, the bound alone decides.
No kernel may reach another device: no remote copies, remote signals or barrier semaphores. Data moves between devices by JAX's collectives and lax.ppermute only.
A program may use at most 64 MiB of HBM per device.

```python
import math
import jax
import jax.numpy as jnp
from jax import lax

DOFS = 64
TRACE = 32
SWEEPS = 2
STEPS_IN = 4
SX = 2
GY = 8
GZ = 16
ELEM_DEV = 256
FACES = 128
ELEMENTS = 4096
INTERVALS = 16
STEPS = 64
N_SPACE = 16


def element_rates(key, lowest, highest):
    key = jax.random.fold_in(key, 11)
    return jax.random.uniform(key, (ELEMENTS,), jnp.float32, lowest, highest)


def block_inverse(key, rates, spread):
    key_gain, key_skew = jax.random.split(key)
    gains = jax.random.uniform(key_gain, (DOFS, ELEMENTS), jnp.float32, 0.9, 1.0) * rates[None, :]
    normals = jax.random.normal(key_skew, (DOFS, DOFS, ELEMENTS), jnp.float32)
    skewed = (normals - jnp.transpose(normals, (1, 0, 2))) * (spread / math.sqrt(2.0)) * rates[None, None, :]
    identity = jnp.eye(DOFS, dtype=jnp.float32)[:, :, None]
    return identity * gains[:, None, :] + skewed


def draw_fine_inverse(key, part):
    rates = element_rates(key, 0.45, 0.9)
    key = jax.random.fold_in(key, 1)
    return block_inverse(key, rates, 0.026)


def draw_coarse_inverse(key, part):
    rates = element_rates(key, 0.45, 0.9)
    key = jax.random.fold_in(key, 2)
    return block_inverse(key, rates * rates, 0.026)


def mesh_orders(key):
    key = jax.random.fold_in(key, 23)
    blocks = ELEMENTS // ELEM_DEV

    def shuffled(sub_key):
        return jax.random.permutation(sub_key, ELEM_DEV).astype(jnp.int32)
    return jax.vmap(shuffled)(jax.random.split(key, blocks))


def draw_neighbour(key, part):
    orders = mesh_orders(key)
    layer = GY * GZ
    position = jnp.arange(ELEM_DEV, dtype=jnp.int32)
    xpos = position // layer
    ypos = position // GZ % GY
    zpos = position % GZ
    face_slot = ypos * GZ + zpos

    def located(xs, ys, zs):
        return orders[:, xs * layer + ys * GZ + zs]
    minus_x = jnp.where(xpos[None, :] > 0, located(jnp.maximum(xpos - 1, 0), ypos, zpos), ELEM_DEV + face_slot[None, :])
    plus_x = jnp.where(xpos[None, :] < SX - 1, located(jnp.minimum(xpos + 1, SX - 1), ypos, zpos), ELEM_DEV + layer + face_slot[None, :])
    minus_y = located(xpos, (ypos + GY - 1) % GY, zpos)
    plus_y = located(xpos, (ypos + 1) % GY, zpos)
    minus_z = located(xpos, ypos, (zpos + GZ - 1) % GZ)
    plus_z = located(xpos, ypos, (zpos + 1) % GZ)
    by_position = jnp.stack([minus_x, plus_x, minus_y, plus_y, minus_z, plus_z]).astype(jnp.int32)
    places = jnp.argsort(orders, axis=1).astype(jnp.int32)
    by_id = jnp.take_along_axis(by_position, jnp.broadcast_to(places[None], by_position.shape), axis=2)
    return by_id.reshape((6, ELEMENTS)).astype(jnp.int32)


def draw_send_low(key, part):
    orders = mesh_orders(key)
    return orders[:, :GY * GZ].reshape((-1,)).astype(jnp.int32)


def draw_send_high(key, part):
    orders = mesh_orders(key)
    return orders[:, (SX - 1) * GY * GZ:].reshape((-1,)).astype(jnp.int32)


def block_scale(rng, shape, cuts, smallest, largest):
    level = 1.0
    for dim, parts in cuts:
        steps = jax.random.uniform(jax.random.fold_in(jax.random.fold_in(rng, 6), dim), (parts,), jnp.float32, smallest / len(cuts), largest / len(cuts))
        level = level * jnp.repeat(jnp.exp(steps), shape[dim] // parts).reshape((-1,) + (1,) * (len(shape) - 1 - dim))
    return level


def scatter_about(rng, extent, scale, most, cuts=(), kind=jnp.bfloat16):
    values = scale * jax.random.normal(rng, extent, jnp.float32)
    if cuts:
        values = values * block_scale(rng, extent, cuts, -0.22, 0.18)
    return jnp.clip(values, -most, most).astype(kind)


def setup_inputs(seed: int = 0) -> dict:
    keys = jax.random.split(jax.random.key(seed), 11)
    return {
        "initial": scatter_about(keys[0], (DOFS, ELEMENTS), 1.0, 6.0, ((1, 16),), jnp.float32),
        "guess": scatter_about(keys[1], (INTERVALS, DOFS, ELEMENTS), 1.0, 6.0, ((0, 16), (2, 16)), jnp.float32),
        "forcing": scatter_about(keys[2], (STEPS, DOFS, ELEMENTS), 0.3, 1.8, ((0, 16), (2, 16)), jnp.float32),
        "fine_inverse": draw_fine_inverse(jax.random.fold_in(keys[10], 71), 0),
        "coarse_inverse": draw_coarse_inverse(jax.random.fold_in(keys[10], 71), 0),
        "neighbour": draw_neighbour(jax.random.fold_in(keys[10], 71), 0),
        "send_low": draw_send_low(jax.random.fold_in(keys[10], 71), 0),
        "send_high": draw_send_high(jax.random.fold_in(keys[10], 71), 0),
        "trace_map": scatter_about(keys[8], (6, TRACE, DOFS), DOFS ** -0.5, 0.75, (), jnp.float32),
        "lift_map": scatter_about(keys[9], (6, DOFS, TRACE), 0.015, 0.09, (), jnp.float32),
    }


HIGH = lax.Precision.HIGHEST


def trace_all(current, trace_map):
    return jnp.einsum('dtj,je->dte', trace_map, current, precision=HIGH)


def outgoing(traces, send_low, send_high):
    return jnp.stack([jnp.take(traces[0], send_low, axis=1), jnp.take(traces[1], send_high, axis=1)])


def couple(traces, from_below, from_above, neighbour, lift_map):
    gathered = []
    for face_index in range(6):
        lookup = jnp.concatenate([traces[face_index ^ 1], from_below, from_above], axis=1)
        gathered.append(jnp.take(lookup, neighbour[face_index], axis=1))
    return jnp.einsum('fit,fte->ie', lift_map, jnp.stack(gathered), precision=HIGH)


def jacobi(right_side, inverse, coupled):
    return jnp.einsum('ije,je->ie', inverse, right_side - coupled, precision=HIGH)


def sweep_mesh(current, right_side, inverse, links, lows, highs, trace_map, lift_map):
    traces = jax.vmap(trace_all, (0, None))(current, trace_map)
    leaving = jax.vmap(outgoing)(traces, lows, highs)
    nothing = jnp.zeros_like(leaving[:1, 0])
    from_below = jnp.concatenate([nothing, leaving[:-1, 1]])
    from_above = jnp.concatenate([leaving[1:, 0], nothing])
    coupled = jax.vmap(couple, (0, 0, 0, 0, None))(traces, from_below, from_above, links, lift_map)
    return jax.vmap(jacobi)(right_side, inverse, coupled)


def to_blocks(array):
    leading = array.shape[:-2]
    reshaped = array.reshape(leading + (DOFS, N_SPACE, ELEM_DEV))
    return jnp.moveaxis(reshaped, -2, -3)


def from_blocks(array):
    moved = jnp.moveaxis(array, -3, -2)
    return moved.reshape(moved.shape[:-3] + (DOFS, ELEMENTS))


def reference(initial, guess, forcing, fine_inverse, coarse_inverse, neighbour, send_low, send_high, trace_map, lift_map):
    start_state = to_blocks(initial)
    guesses = to_blocks(guess)
    forces = to_blocks(forcing).reshape((INTERVALS, STEPS_IN, N_SPACE, DOFS, ELEM_DEV))
    fine_blocks = jnp.moveaxis(fine_inverse.reshape((DOFS, DOFS, N_SPACE, ELEM_DEV)), 2, 0)
    coarse_blocks = jnp.moveaxis(coarse_inverse.reshape((DOFS, DOFS, N_SPACE, ELEM_DEV)), 2, 0)
    links = jnp.moveaxis(neighbour.reshape((6, N_SPACE, ELEM_DEV)), 1, 0)
    lows = send_low.reshape((N_SPACE, FACES))
    highs = send_high.reshape((N_SPACE, FACES))

    def propagate(current, right_side, inverse):
        updated = current
        for sweep_index in range(SWEEPS):
            updated = sweep_mesh(updated, right_side, inverse, links, lows, highs, trace_map, lift_map)
        return updated

    def fine_step(current, forcing_now):
        return propagate(current, current + forcing_now, fine_blocks)

    stepped = jax.vmap(fine_step)

    def previous(end_states):
        return jnp.concatenate([start_state[None], end_states[:-1]])

    def relax(anchor):
        points = []
        current = anchor
        for inner_step in range(STEPS_IN - 1):
            current = stepped(current, forces[:, inner_step])
            points.append(current)
        return points

    first_pass = relax(previous(guesses))
    residual = stepped(first_pass[-1], forces[:, STEPS_IN - 1]) - guesses

    def coarse_turn(carried, residual_now):
        corrected = propagate(carried, carried, coarse_blocks) + residual_now
        return corrected, corrected

    last_carry, correction = lax.scan(coarse_turn, jnp.zeros_like(start_state), residual)
    final_end = guesses + correction
    last_pass = relax(previous(final_end))
    result = jnp.stack(last_pass + [final_end], axis=1)
    return from_blocks(result.reshape((STEPS, N_SPACE, DOFS, ELEM_DEV)))
```

```python
import functools

import jax
import jax.numpy as jnp
from jax import lax
from jax.experimental import pallas as pl
from jax.experimental.pallas import tpu as pltpu
from jax.sharding import PartitionSpec as P

DOFS = 64
TRACE = 32
LANES = 128
ELEMS = 256
F32 = jnp.float32
BF16 = jnp.bfloat16

VMEM = pl.BlockSpec(memory_space=pltpu.VMEM)
SMEM = pl.BlockSpec(memory_space=pltpu.SMEM)


def halves(x):
    high = x.astype(BF16)
    return high, (x - high.astype(F32)).astype(BF16)


def dot(a, b):
    return jnp.dot(a, b, preferred_element_type=F32)


def dot3(weights, x):
    high, low = halves(x)
    return dot(weights, jnp.concatenate([high, low, high], axis=0))


def split_weights(w):
    high, low = halves(w)
    return jnp.concatenate([high.astype(F32), high.astype(F32), low.astype(F32)], axis=1).astype(BF16)


def pick(source, lane):
    return jnp.take_along_axis(source, lane, axis=1, mode="promise_in_bounds")


def pick_wide(source, index):
    rows = source.shape[0]
    index = jnp.broadcast_to(index, (rows, LANES))
    lane = index & (LANES - 1)
    return jnp.where(index < LANES, pick(source[:, :LANES], lane), pick(source[:, LANES:], lane))


def gathered(traces, below, above, nbr_ref):
    rows = []
    for face in range(6):
        first = (face ^ 1) * TRACE
        source = traces[first : first + TRACE]
        parts = []
        for half in range(2):
            index = nbr_ref[face : face + 1, half * LANES : (half + 1) * LANES]
            index = jnp.broadcast_to(index, (TRACE, LANES))
            lane = index & (LANES - 1)
            value = jnp.where(index < LANES, pick(source[:, :LANES], lane), pick(source[:, LANES:], lane))
            if face < 2:
                outer = (below, above)[face]
                other = jnp.zeros((TRACE, LANES), F32) if outer is None else pick(outer, lane)
                value = jnp.where(index < 2 * LANES, value, other)
            parts.append(value)
        rows.append(jnp.concatenate(parts, axis=1))
    return jnp.concatenate(rows, axis=0)


def boundary(below, above, nbr_ref):
    rows = []
    for face, outer in enumerate((below, above)):
        parts = []
        for half in range(2):
            index = nbr_ref[face : face + 1, half * LANES : (half + 1) * LANES]
            index = jnp.broadcast_to(index, (TRACE, LANES))
            parts.append(jnp.where(index < 2 * LANES, 0.0, pick(outer, index & (LANES - 1))))
        rows.append(jnp.concatenate(parts, axis=1))
    return jnp.concatenate(rows, axis=0)


def apply_inverse(q_ref, d_ref, rows_ref, right):
    rows_ref[...] = right

    def step(chunk, total):
        for k in range(8):
            j = chunk * 8 + k
            total = total - q_ref[j] * rows_ref[pl.ds(j, 1), :]
        return total

    return lax.fori_loop(0, DOFS // 8, step, 2.0 * d_ref[...] * right)


def apply_faces(k_ref, rows_ref, right):
    rows_ref[...] = right

    def step(chunk, total):
        for k in range(8):
            u = chunk * 8 + k
            total = total + k_ref[u] * rows_ref[pl.ds(u, 1), :]
        return total

    return lax.fori_loop(0, TRACE // 8, step, jnp.zeros((TRACE, LANES), F32))


def weights_kernel(trace_ref, lift_ref, wt_ref, wl_ref, wi_ref):
    wt_ref[...] = split_weights(trace_ref[...])
    wl_ref[...] = split_weights(lift_ref[...])
    wi_ref[...] = split_weights(lift_ref[:, : 2 * TRACE])


def faces_kernel(q_ref, send_ref, tr_ref, lift_ref, d_ref, k0_ref, k1_ref, m0_ref, m1_ref):
    for i in range(DOFS):
        d_ref[i : i + 1, :] = q_ref[i, i : i + 1, :]
    tr = split_weights(tr_ref[...])
    lifts = [split_weights(lift_ref[slot]) for slot in range(2)]
    column = lax.broadcasted_iota(jnp.int32, (2 * TRACE, DOFS), 1)

    def maps(j, carry):
        here = jnp.sum(jnp.where(column == j, tr_ref[...], 0.0), axis=1, keepdims=True)
        m = 2.0 * here * d_ref[pl.ds(j, 1), :] - dot3(tr, q_ref[j])
        place = pl.ds(pl.multiple_of(j * TRACE, TRACE), TRACE)
        m0_ref[place, :] = pick_wide(m[:TRACE], send_ref[0:1, :])
        m1_ref[place, :] = pick_wide(m[TRACE:], send_ref[1:2, :])
        return carry

    lax.fori_loop(0, DOFS, maps, 0, unroll=4)

    def lift(t, carry):
        for m_ref, k_ref, w in ((m0_ref, k0_ref, lifts[0]), (m1_ref, k1_ref, lifts[1])):
            rows = m_ref[pl.ds(t, DOFS, stride=TRACE), :]
            k_ref[pl.ds(t, TRACE, stride=TRACE), :] = dot3(w, rows)
        return carry

    lax.fori_loop(0, TRACE, lift, 0, unroll=4)


def sides(scal_ref, first, second):
    even = scal_ref[0] == 0
    return jnp.where(even, second, first), jnp.where(even, first, second)


def finish(scal_ref, w, rec0_ref, rec1_ref, g_ref, b_ref, x_ref, rows_ref, face_rows_ref):
    q_ref, d_ref, k0_ref, k1_ref, nbr_ref, send_ref, wt_ref, wl_ref, wi_ref = w
    there = scal_ref[1] == 1
    rec0 = rec0_ref[...]
    rec1 = jnp.where(there, rec1_ref[...], 0.0)
    below, above = sides(scal_ref, rec0[TRACE:], rec1[TRACE:])
    outer = dot3(wi_ref[...], boundary(below, above, nbr_ref))
    v1 = apply_inverse(q_ref, d_ref, rows_ref, g_ref[...] - outer)
    traces = dot3(wt_ref[...], v1)
    next0 = rec0[:TRACE] - apply_faces(k0_ref, face_rows_ref, x_ref[:TRACE])
    next1 = rec1[:TRACE] - apply_faces(k1_ref, face_rows_ref, x_ref[TRACE:])
    below, above = sides(scal_ref, next0, jnp.where(there, next1, 0.0))
    coupled = dot3(wl_ref[...], gathered(traces, below, above, nbr_ref))
    return apply_inverse(q_ref, d_ref, rows_ref, b_ref[...] - coupled)


def begin(scal_ref, w, v, b, g_ref, x_ref, msg0_ref, msg1_ref, rows_ref):
    q_ref, d_ref, nbr_ref, send_ref, wt_ref, wl_ref = w
    even = scal_ref[0] == 0

    def leaving(traces):
        low, high = traces[:TRACE], traces[TRACE : 2 * TRACE]
        return (
            pick_wide(jnp.where(even, high, low), send_ref[0:1, :]),
            pick_wide(jnp.where(even, low, high), send_ref[1:2, :]),
        )

    traces = dot3(wt_ref[...], v)
    x0, x1 = leaving(traces)
    g = b - dot3(wl_ref[...], gathered(traces, None, None, nbr_ref))
    u = apply_inverse(q_ref, d_ref, rows_ref, g)
    w0, w1 = leaving(dot3(wt_ref[: 2 * TRACE, :], u))
    g_ref[...] = g
    x_ref[...] = jnp.concatenate([x0, x1], axis=0)
    msg0_ref[...] = jnp.concatenate([w0, x0], axis=0)
    msg1_ref[...] = jnp.concatenate([w1, x1], axis=0)


def first_kernel(scal_ref, q_ref, d_ref, nbr_ref, send_ref, wt_ref, wl_ref, anchor_ref, force_ref,
                 b_ref, g_ref, x_ref, msg0_ref, msg1_ref, rows_ref):
    v = anchor_ref[...]
    b = v + force_ref[0]
    b_ref[...] = b
    begin(scal_ref, (q_ref, d_ref, nbr_ref, send_ref, wt_ref, wl_ref), v, b, g_ref, x_ref, msg0_ref, msg1_ref, rows_ref)


def fine_kernel(step, scal_ref, q_ref, d_ref, k0_ref, k1_ref, nbr_ref, send_ref, wt_ref, wl_ref, wi_ref,
                rec0_ref, rec1_ref, bin_ref, gin_ref, xin_ref, force_ref,
                v_ref, b_ref, g_ref, x_ref, msg0_ref, msg1_ref, rows_ref, face_rows_ref):
    op = (q_ref, d_ref, k0_ref, k1_ref, nbr_ref, send_ref, wt_ref, wl_ref, wi_ref)
    v = finish(scal_ref, op, rec0_ref, rec1_ref, gin_ref, bin_ref, xin_ref, rows_ref, face_rows_ref)
    v_ref[...] = v
    b = v + force_ref[step]
    b_ref[...] = b
    begin(scal_ref, (q_ref, d_ref, nbr_ref, send_ref, wt_ref, wl_ref), v, b, g_ref, x_ref, msg0_ref, msg1_ref, rows_ref)


def last_kernel(scal_ref, q_ref, d_ref, k0_ref, k1_ref, nbr_ref, send_ref, wt_ref, wl_ref, wi_ref,
                rec0_ref, rec1_ref, bin_ref, gin_ref, xin_ref, less_ref, v_ref, rows_ref, face_rows_ref):
    op = (q_ref, d_ref, k0_ref, k1_ref, nbr_ref, send_ref, wt_ref, wl_ref, wi_ref)
    v = finish(scal_ref, op, rec0_ref, rec1_ref, gin_ref, bin_ref, xin_ref, rows_ref, face_rows_ref)
    v_ref[...] = v - less_ref[...]


def start_kernel(scal_ref, q_ref, d_ref, nbr_ref, send_ref, wt_ref, wl_ref, v_ref,
                 g_ref, x_ref, msg0_ref, msg1_ref, rows_ref):
    v = v_ref[...]
    begin(scal_ref, (q_ref, d_ref, nbr_ref, send_ref, wt_ref, wl_ref), v, v, g_ref, x_ref, msg0_ref, msg1_ref, rows_ref)


def turn_kernel(turn, more, scal_ref, q_ref, d_ref, k0_ref, k1_ref, nbr_ref, send_ref, wt_ref, wl_ref, wi_ref,
                rec0_ref, rec1_ref, bin_ref, gin_ref, xin_ref, res_ref, *refs):
    if more:
        b_ref, g_ref, x_ref, msg0_ref, msg1_ref, rows_ref, face_rows_ref = refs
    else:
        b_ref, rows_ref, face_rows_ref = refs
    op = (q_ref, d_ref, k0_ref, k1_ref, nbr_ref, send_ref, wt_ref, wl_ref, wi_ref)
    v = finish(scal_ref, op, rec0_ref, rec1_ref, gin_ref, bin_ref, xin_ref, rows_ref, face_rows_ref)
    v = v + res_ref[scal_ref[2 + turn]]
    b_ref[...] = v
    if more:
        begin(scal_ref, (q_ref, d_ref, nbr_ref, send_ref, wt_ref, wl_ref), v, v, g_ref, x_ref, msg0_ref, msg1_ref, rows_ref)


def shape(*dims, dtype=F32):
    return jax.ShapeDtypeStruct(dims, dtype)


STATE = shape(DOFS, ELEMS)
EDGE = shape(2 * TRACE, LANES)
ROWS = pltpu.VMEM((DOFS, ELEMS), F32)
FACE_ROWS = pltpu.VMEM((TRACE, LANES), F32)
BEGUN = (STATE, EDGE, EDGE, EDGE)


def call(kernel, outs, scratch, *args, scalars=True, limit=None, cost=None):
    specs = [VMEM] * len(args)
    if scalars:
        specs[0] = SMEM
    return pl.pallas_call(
        kernel,
        out_shape=outs,
        in_specs=specs,
        out_specs=[VMEM] * len(outs),
        scratch_shapes=scratch,
        compiler_params=pltpu.CompilerParams(vmem_limit_bytes=limit),
    )(*args)


def local(
    initial,
    guess,
    forcing,
    fine_inverse,
    coarse_inverse,
    neighbour,
    send_low,
    send_high,
    trace_map,
    lift_map,
):
    times = lax.axis_size("tm")
    blocks = lax.axis_size("space")
    now = lax.axis_index("tm")
    place = lax.axis_index("space")
    odd = place % 2
    guess = guess[0]

    def route(time_of, place_of):
        return [
            (t * blocks + s, time_of(t) * blocks + place_of(s))
            for t in range(times)
            for s in range(blocks)
        ]

    def other(s):
        there = s + 1 if s % 2 else s - 1
        return there if 0 <= there < blocks else s

    same = lambda i: i
    beside = [route(same, lambda s: s ^ 1), route(same, other)]

    def move(x, pairs):
        return lax.ppermute(x, ("tm", "space"), pairs)

    def exchange(first, second):
        return move(first, beside[0]), move(second, beside[1])

    def by_partner(low, high):
        return jnp.where(odd == 0, jnp.stack([high, low]), jnp.stack([low, high]))

    send = by_partner(send_low, send_high)
    tr = by_partner(trace_map[0], trace_map[1]).reshape(2 * TRACE, DOFS)
    lift_sides = by_partner(lift_map[0].T, lift_map[1].T)
    has_second = jnp.where(odd == 0, place > 0, place < blocks - 1).astype(jnp.int32)
    group, core = now % 8 // 2, now % 2
    turns = jnp.arange(8)
    slots = ((group - turns // 2) % 4) * 2 + (turns % 2 ^ core)
    scal = jnp.concatenate([jnp.stack([odd, has_second]), slots]).astype(jnp.int32)

    wt, wl, wi = call(
        weights_kernel,
        [shape(192, 192, dtype=BF16), shape(64, 576, dtype=BF16), shape(64, 192, dtype=BF16)],
        [],
        trace_map.reshape(6 * TRACE, DOFS),
        jnp.transpose(lift_map, (1, 0, 2)).reshape(DOFS, 6 * TRACE),
        scalars=False,
    )

    def operator(inverse):
        d, k0, k1 = call(
            faces_kernel,
            [STATE, shape(TRACE * TRACE, LANES), shape(TRACE * TRACE, LANES)],
            [pltpu.VMEM((DOFS * TRACE, LANES), F32)] * 2,
            inverse,
            send,
            tr,
            lift_sides,
            scalars=False,
        )
        k0, k1 = exchange(k0, k1)
        return inverse, d, k0.reshape(TRACE, TRACE, LANES), k1.reshape(TRACE, TRACE, LANES)

    ahead = [(i, i + 1) for i in range(times - 1)]
    moved = lax.ppermute(guess, "tm", ahead)
    anchor = jnp.where(now == 0, initial, moved)
    fine = operator(fine_inverse)
    coarse = operator(coarse_inverse)
    short = (neighbour, send, wt, wl)
    tables = (neighbour, send, wt, wl, wi)

    def relax(start, count, less):
        b, g, x, m0, m1 = call(
            first_kernel, [STATE, *BEGUN], [ROWS], scal, *fine[:2], *short, start, forcing
        )
        points = []
        for step in range(1, count):
            m0, m1 = exchange(m0, m1)
            v, b, g, x, m0, m1 = call(
                functools.partial(fine_kernel, step),
                [STATE, STATE, *BEGUN],
                [ROWS, FACE_ROWS],
                scal, *fine, *tables, m0, m1, b, g, x, forcing,
            )
            points.append(v)
        m0, m1 = exchange(m0, m1)
        (v,) = call(
            last_kernel, [STATE], [ROWS, FACE_ROWS], scal, *fine, *tables, m0, m1, b, g, x, less
        )
        return points + [v]

    residual = relax(anchor, 4, guess)[-1]
    partner_core = route(lambda t: t ^ 1, same)
    pair = jnp.stack([residual, move(residual, partner_core)])

    def turned(k):
        return route(lambda t: t // 8 * 8 + (t % 8 + 2 * k) % 8, same)

    held = jnp.concatenate([pair] + [move(pair, turned(k)) for k in (1, 2, 3)])

    def chain(b, first, count):
        g, x, m0, m1 = call(start_kernel, BEGUN, [ROWS], scal, *coarse[:2], *short, b)
        ends = [b]
        for turn in range(first, first + count):
            more = turn < first + count - 1
            m0, m1 = exchange(m0, m1)
            out = call(
                functools.partial(turn_kernel, turn, more),
                [STATE, *BEGUN] if more else [STATE],
                [ROWS, FACE_ROWS],
                scal, *coarse, *tables, m0, m1, b, g, x, held,
            )
            b = out[0]
            if more:
                b, g, x, m0, m1 = out
            ends.append(b)
        return ends

    early = now < 8
    turn = now % 8
    base = lax.dynamic_index_in_dim(held, scal[2], 0, False)
    early_ends = chain(base, 1, 7)
    late_ends = chain(move(early_ends[-1], route(lambda t: t ^ 8, same)), 0, 8)
    zero = jnp.zeros_like(base)
    before = jnp.where(early, jnp.where(turn == 0, zero, 0.0), late_ends[0])
    after = jnp.where(early, early_ends[0], late_ends[1])
    for k in range(1, 8):
        before = jnp.where(turn == k, jnp.where(early, early_ends[k - 1], late_ends[k]), before)
        after = jnp.where(turn == k, jnp.where(early, early_ends[k], late_ends[k + 1]), after)
    last_pass = relax(anchor + before, 3, zero)
    return jnp.stack(last_pass + [guess + after])


def solution(mesh):
    in_specs = (
        P(None, "space"),
        P("tm", None, "space"),
        P("tm", None, "space"),
        P(None, None, "space"),
        P(None, None, "space"),
        P(None, "space"),
        P("space"),
        P("space"),
        P(),
        P(),
    )
    out_specs = P("tm", None, "space")
    return jax.shard_map(local, mesh=mesh, in_specs=in_specs, out_specs=out_specs, check_vma=False)
```

```python
import functools

import jax
import jax.numpy as jnp
from jax import lax
from jax.experimental import pallas as pl
from jax.experimental.pallas import tpu as pltpu
from jax.sharding import PartitionSpec as P

DOFS = 64
TRACE = 32
LANES = 128
ELEMS = 256
HALF = 8
F32 = jnp.float32
BF16 = jnp.bfloat16

VMEM = pl.BlockSpec(memory_space=pltpu.VMEM)
SMEM = pl.BlockSpec(memory_space=pltpu.SMEM)


def halves(x):
    high = x.astype(BF16)
    return high, (x - high.astype(F32)).astype(BF16)


def dot(a, b):
    return jnp.dot(a, b, preferred_element_type=F32)


def dot3(weights, x):
    high, low = halves(x)
    return dot(weights, jnp.concatenate([high, low, high], axis=0))


def split_weights(w):
    high, low = halves(w)
    return jnp.concatenate([high.astype(F32), high.astype(F32), low.astype(F32)], axis=1).astype(BF16)


def pick(source, lane):
    lane = jnp.broadcast_to(lane, source.shape)
    return jnp.take_along_axis(source, lane, axis=1, mode="promise_in_bounds")


def pick_wide(source, index):
    lane = index & (LANES - 1)
    first, second = pick(source[:, :LANES], lane), pick(source[:, LANES:], lane)
    return jnp.where(jnp.broadcast_to(index, first.shape) < LANES, first, second)


def reorder(source, index_ref):
    return jnp.concatenate([pick_wide(source, index_ref[0:1, :]), pick_wide(source, index_ref[1:2, :])], axis=1)


def gathered(traces, below, above, near_ref):
    nothing = jnp.zeros((TRACE, LANES), F32)
    rows = []
    for face in range(6):
        first = (face ^ 1) * TRACE
        low = traces[first : first + TRACE, :LANES]
        high = traces[first : first + TRACE, LANES:]
        if face == 0:
            pair = [nothing if below is None else below, pick(low, near_ref[0:1, :])]
        elif face == 1:
            pair = [pick(high, near_ref[1:2, :]), nothing if above is None else above]
        else:
            pair = [pick(low, near_ref[2 * face - 2 : 2 * face - 1, :]), pick(high, near_ref[2 * face - 1 : 2 * face, :])]
        rows.append(jnp.concatenate(pair, axis=1))
    return jnp.concatenate(rows, axis=0)


def apply_inverse(q_ref, d_ref, rows_ref, right):
    rows_ref[...] = right

    def step(chunk, total):
        for k in range(8):
            j = chunk * 8 + k
            total = total - q_ref[j] * rows_ref[pl.ds(j, 1), :]
        return total

    return lax.fori_loop(0, DOFS // 8, step, 2.0 * d_ref[...] * right)


def apply_faces(k_ref, rows_ref, right):
    rows_ref[...] = right

    def step(chunk, total):
        for k in range(8):
            u = chunk * 8 + k
            block = k_ref[pl.ds(pl.multiple_of(u * TRACE, TRACE), TRACE), :]
            total = total + block * rows_ref[pl.ds(u, 1), :]
        return total

    return lax.fori_loop(0, TRACE // 8, step, jnp.zeros((TRACE, LANES), F32))


def tables_kernel(trace_ref, lift_ref, nbr_ref, send_ref, wt_ref, wl_ref, wi_ref, near_ref, back_ref):
    wt_ref[...] = split_weights(trace_ref[...])
    wl_ref[...] = split_weights(lift_ref[...])
    wi_ref[0] = split_weights(lift_ref[:, :TRACE])
    wi_ref[1] = split_weights(lift_ref[:, TRACE : 2 * TRACE])
    position = lax.broadcasted_iota(jnp.int32, (LANES, LANES), 0)
    lane = lax.broadcasted_iota(jnp.int32, (LANES, LANES), 1)
    places = []
    for half in range(2):
        place = jnp.zeros((1, LANES), F32)
        for layer in range(2):
            ids = jnp.broadcast_to(send_ref[layer : layer + 1, :], (LANES, LANES)).astype(F32)
            ids = jnp.transpose(ids).astype(jnp.int32)
            here = jnp.where(ids == lane + half * LANES, position + layer * LANES, 0).astype(F32)
            place = place + jnp.sum(here, axis=0, keepdims=True)
        places.append(place.astype(jnp.int32))
    back_ref[0:1, :] = places[0]
    back_ref[1:2, :] = places[1]
    place = jnp.broadcast_to(jnp.concatenate(places, axis=1), (8, ELEMS))
    order = [(0, 1), (1, 0)] + [(face, layer) for face in range(2, 6) for layer in range(2)]
    for row, (face, layer) in enumerate(order):
        ids = pick_wide(jnp.broadcast_to(nbr_ref[face : face + 1, :], (8, ELEMS)), send_ref[layer : layer + 1, :])
        near_ref[row : row + 1, :] = (pick_wide(place, ids[0:1]) & (LANES - 1))[0:1]


def prepare_kernel(q_ref, send_ref, tr_ref, lift_ref, out_ref, d_ref, klow_ref, khigh_ref, mlow_ref, mhigh_ref):
    tr = split_weights(tr_ref[...])
    lift = split_weights(lift_ref[...])
    column = lax.broadcasted_iota(jnp.int32, (2 * TRACE, DOFS), 1)

    def maps(j, carry):
        q = reorder(q_ref[j], send_ref)
        out_ref[j] = q
        row = out_ref[j, pl.ds(j, 1), :]
        d_ref[pl.ds(j, 1), :] = row
        here = jnp.sum(jnp.where(column == j, tr_ref[...], 0.0), axis=1, keepdims=True)
        m = 2.0 * here * row - dot3(tr, q)
        place = pl.ds(pl.multiple_of(j * TRACE, TRACE), TRACE)
        mlow_ref[place, :] = m[:TRACE, :LANES]
        mhigh_ref[place, :] = m[TRACE:, LANES:]
        return carry

    lax.fori_loop(0, DOFS, maps, 0, unroll=4)

    def lifts(t, carry):
        rows = pl.ds(t, DOFS, stride=TRACE)
        k = dot3(lift, jnp.concatenate([mlow_ref[rows, :], mhigh_ref[rows, :]], axis=1))
        klow_ref[pl.ds(t, TRACE, stride=TRACE), :] = k[:TRACE, :LANES]
        khigh_ref[pl.ds(t, TRACE, stride=TRACE), :] = k[TRACE:, LANES:]
        return carry

    lax.fori_loop(0, TRACE, lifts, 0, unroll=4)


def reorder_kernel(force_ref, guess_ref, send_ref, force_out_ref, guess_out_ref):
    for step in range(4):
        force_out_ref[step] = reorder(force_ref[step], send_ref)
    guess_out_ref[...] = reorder(guess_ref[...], send_ref)


def finish(scal_ref, w, below_ref, above_ref, first, g_ref, b_ref, kx_ref, rows_ref):
    q_ref, d_ref, near_ref, wt_ref, wl_ref, wi_ref = w
    below = jnp.where(scal_ref[0] == 1, below_ref[first : first + 2 * TRACE, :], 0.0)
    above = jnp.where(scal_ref[1] == 1, above_ref[first : first + 2 * TRACE, :], 0.0)
    outer = jnp.concatenate([dot3(wi_ref[0], below[TRACE:]), dot3(wi_ref[1], above[TRACE:])], axis=1)
    v1 = apply_inverse(q_ref, d_ref, rows_ref, g_ref[...] - outer)
    traces = dot3(wt_ref[...], v1)
    below = below[:TRACE] - kx_ref[:TRACE, :]
    above = above[:TRACE] - kx_ref[TRACE:, :]
    coupled = dot3(wl_ref[...], gathered(traces, below, above, near_ref))
    return apply_inverse(q_ref, d_ref, rows_ref, b_ref[...] - coupled)


def begin(w, v, b, outs, rows_ref):
    q_ref, d_ref, near_ref, wt_ref, wl_ref, wi_ref = w
    b_ref, g_ref, low_ref, high_ref = outs
    traces = dot3(wt_ref[...], v)
    g = b - dot3(wl_ref[...], gathered(traces, None, None, near_ref))
    u = apply_inverse(q_ref, d_ref, rows_ref, g)
    ends = dot3(wt_ref[: 2 * TRACE, :], u)
    b_ref[...] = b
    g_ref[...] = g
    low_ref[:TRACE, :] = ends[:TRACE, :LANES]
    low_ref[TRACE:, :] = traces[:TRACE, :LANES]
    high_ref[:TRACE, :] = ends[TRACE:, LANES:]
    high_ref[TRACE:, :] = traces[TRACE : 2 * TRACE, LANES:]


def cross_kernel(scal_ref, kbelow_ref, kabove_ref, low_ref, high_ref, kx_ref, rows_ref):
    below = apply_faces(kbelow_ref, rows_ref, low_ref[TRACE:, :])
    above = apply_faces(kabove_ref, rows_ref, high_ref[TRACE:, :])
    kx_ref[:TRACE, :] = jnp.where(scal_ref[0] == 1, below, 0.0)
    kx_ref[TRACE:, :] = jnp.where(scal_ref[1] == 1, above, 0.0)


def first_kernel(q_ref, d_ref, near_ref, wt_ref, wl_ref, wi_ref, anchor_ref, send_ref, force_ref, v_ref, *outs):
    v = reorder(anchor_ref[...], send_ref)
    v_ref[...] = v
    begin((q_ref, d_ref, near_ref, wt_ref, wl_ref, wi_ref), v, v + force_ref[0], outs[:4], outs[4])


def again_kernel(scal_ref, q_ref, d_ref, near_ref, wt_ref, wl_ref, wi_ref, anchor_ref, force_ref, *refs):
    ends, outs = refs[:-5], refs[-5:]
    turn = scal_ref[2]
    before = jnp.zeros((DOFS, ELEMS), F32)
    for k, end_ref in enumerate(ends):
        before = jnp.where(turn == k, end_ref[...], before)
    v = anchor_ref[...] + before
    begin((q_ref, d_ref, near_ref, wt_ref, wl_ref, wi_ref), v, v + force_ref[0], outs[:4], outs[4])


def fine_kernel(step, scal_ref, q_ref, d_ref, near_ref, wt_ref, wl_ref, wi_ref,
                below_ref, above_ref, bin_ref, gin_ref, kx_ref, force_ref, v_ref, *outs):
    w = (q_ref, d_ref, near_ref, wt_ref, wl_ref, wi_ref)
    v = finish(scal_ref, w, below_ref, above_ref, 0, gin_ref, bin_ref, kx_ref, outs[4])
    v_ref[...] = v
    begin(w, v, v + force_ref[step], outs[:4], outs[4])


def residual_kernel(scal_ref, q_ref, d_ref, near_ref, wt_ref, wl_ref, wi_ref,
                    below_ref, above_ref, bin_ref, gin_ref, kx_ref, guess_ref, v_ref, rows_ref):
    w = (q_ref, d_ref, near_ref, wt_ref, wl_ref, wi_ref)
    v = finish(scal_ref, w, below_ref, above_ref, 0, gin_ref, bin_ref, kx_ref, rows_ref)
    v_ref[...] = v - guess_ref[...]


def last_kernel(scal_ref, q_ref, d_ref, near_ref, wt_ref, wl_ref, wi_ref,
                below_ref, above_ref, bin_ref, gin_ref, kx_ref, guess_ref, back_ref, v1_ref, v2_ref, *refs):
    ends, (out_ref, rows_ref) = refs[:-2], refs[-2:]
    w = (q_ref, d_ref, near_ref, wt_ref, wl_ref, wi_ref)
    v = finish(scal_ref, w, below_ref, above_ref, 0, gin_ref, bin_ref, kx_ref, rows_ref)
    out_ref[0] = reorder(v1_ref[...], back_ref)
    out_ref[1] = reorder(v2_ref[...], back_ref)
    out_ref[2] = reorder(v, back_ref)
    turn = scal_ref[3]
    after = jnp.zeros((DOFS, ELEMS), F32)
    for k, end_ref in enumerate(ends):
        after = jnp.where(turn == k, end_ref[...], after)
    out_ref[3] = reorder(guess_ref[...] + after, back_ref)


def start_kernel(q_ref, d_ref, near_ref, wt_ref, wl_ref, wi_ref, v_ref, *outs):
    v = v_ref[...]
    begin((q_ref, d_ref, near_ref, wt_ref, wl_ref, wi_ref), v, v, outs[:4], outs[4])


def turn_kernel(turn, first, more, scal_ref, q_ref, d_ref, near_ref, wt_ref, wl_ref, wi_ref,
                below_ref, above_ref, bin_ref, gin_ref, kx_ref, res_ref, *outs):
    w = (q_ref, d_ref, near_ref, wt_ref, wl_ref, wi_ref)
    v = finish(scal_ref, w, below_ref, above_ref, first, gin_ref, bin_ref, kx_ref, outs[-1])
    v = v + res_ref[scal_ref[4 + turn]]
    if more:
        begin(w, v, v, outs[:4], outs[4])
    else:
        outs[0][...] = v


STATE = ((DOFS, ELEMS), F32)
EDGE = ((2 * TRACE, LANES), F32)
FACES = ((TRACE * TRACE, LANES), F32)
ROWS = pltpu.VMEM((DOFS, ELEMS), F32)
FACE_ROWS = pltpu.VMEM((TRACE, LANES), F32)
BEGUN = (STATE, STATE, EDGE, EDGE)


def call(kernel, outs, scratch, *args, scalars=True, hbm_out=False):
    specs = [VMEM] * len(args)
    first = 1 if scalars else 0
    if scalars:
        specs[0] = SMEM
    args = args[:first] + tuple(pltpu.with_memory_space_constraint(x, pltpu.VMEM) for x in args[first:])
    kind = jax.ShapeDtypeStruct if hbm_out else pltpu.VMEM
    return pl.pallas_call(
        kernel,
        out_shape=[kind(*x) for x in outs],
        in_specs=specs,
        out_specs=[VMEM] * len(outs),
        scratch_shapes=scratch,
        compiler_params=pltpu.CompilerParams(vmem_limit_bytes=8 << 20),
    )(*args)


def local(
    initial,
    guess,
    forcing,
    fine_inverse,
    coarse_inverse,
    neighbour,
    send_low,
    send_high,
    trace_map,
    lift_map,
):
    times = lax.axis_size("tm")
    blocks = lax.axis_size("space")
    now = lax.axis_index("tm")
    place = lax.axis_index("space")
    guess = guess[0]

    def route(target):
        return [
            (t * blocks + s, a * blocks + b)
            for t in range(times)
            for s in range(blocks)
            for a, b in [target(t, s)]
        ]

    def shift(by):
        def target(t, s):
            there = s + by
            return (t, there) if 0 <= there < blocks else ((t + HALF) % times, there % blocks)

        return route(target)

    up, down = shift(1), shift(-1)

    def move(x, pairs):
        return lax.ppermute(x, ("tm", "space"), pairs)

    def exchange(low, high):
        above = move(low, down)
        below = move(high, up)
        return below, above

    group, core = now % HALF // 2, now % 2
    turns = jnp.arange(HALF)
    slots = ((group - turns // 2) % 4) * 2 + (turns % 2 ^ core)
    early = now < HALF
    turn = now % HALF
    before = jnp.where(early, turn - 1, HALF + turn)
    after = jnp.where(early, turn, HALF + turn + 1)
    scal = jnp.concatenate([jnp.stack([place > 0, place < blocks - 1, before, after]), slots]).astype(jnp.int32)

    send = jnp.stack([send_low, send_high])
    ahead = [(i, i + 1) for i in range(times - 1)]
    moved = lax.ppermute(guess, "tm", ahead)
    wt, wl, wi, near, back = call(
        tables_kernel,
        [((192, 192), BF16), ((64, 576), BF16), ((2, 64, 96), BF16), ((16, LANES), jnp.int32), ((2, LANES), jnp.int32)],
        [],
        trace_map.reshape(6 * TRACE, DOFS),
        jnp.transpose(lift_map, (1, 0, 2)).reshape(DOFS, 6 * TRACE),
        neighbour,
        send,
        scalars=False,
    )
    outer_trace = trace_map[:2].reshape(2 * TRACE, DOFS)
    outer_lift = jnp.transpose(lift_map[:2], (0, 2, 1)).reshape(2 * TRACE, DOFS)

    def operator(inverse):
        q, d, klow, khigh = call(
            prepare_kernel,
            [((DOFS, DOFS, ELEMS), F32), STATE, FACES, FACES],
            [pltpu.VMEM((DOFS * TRACE, LANES), F32)] * 2,
            inverse, send, outer_trace, outer_lift,
            scalars=False,
        )
        return (q, d, near, wt, wl, wi), exchange(klow, khigh)

    def cross(faces, low, high):
        (kx,) = call(cross_kernel, [EDGE], [FACE_ROWS], scal, *faces, low, high)
        return kx

    fine, fine_faces = operator(fine_inverse)
    forces, ends = call(reorder_kernel, [((4, DOFS, ELEMS), F32), STATE], [], forcing, guess, send, scalars=False)
    coarse, coarse_faces = operator(coarse_inverse)
    anchor, b, g, low, high = call(
        first_kernel, [STATE, *BEGUN], [ROWS], *fine, jnp.where(now == 0, initial, moved), send, forces, scalars=False
    )

    def fine_step(step, b, g, low, high):
        kx = cross(fine_faces, low, high)
        below, above = exchange(low, high)
        return call(
            functools.partial(fine_kernel, step), [STATE, *BEGUN], [ROWS],
            scal, *fine, below, above, b, g, kx, forces,
        )

    for step in (1, 2, 3):
        _, b, g, low, high = fine_step(step, b, g, low, high)
    kx = cross(fine_faces, low, high)
    below, above = exchange(low, high)
    (residual,) = call(residual_kernel, [STATE], [ROWS], scal, *fine, below, above, b, g, kx, ends)

    pair = jnp.stack([residual, move(residual, route(lambda t, s: (t ^ 1, s)))])

    def turned(k):
        return route(lambda t, s: (t // HALF * HALF + (t % HALF + 2 * k) % HALF, s))

    held = jnp.concatenate([pair] + [move(pair, turned(k)) for k in (1, 2, 3)])

    def chain(b, first, count):
        b, g, low, high = call(start_kernel, BEGUN, [ROWS], *coarse, b, scalars=False)
        ends = [b]
        for turn in range(first, first + count):
            kx = cross(coarse_faces, low, high)
            below, above = exchange(low, high)
            b, g, low, high = call(
                functools.partial(turn_kernel, turn, 0, True), BEGUN, [ROWS],
                scal, *coarse, below, above, b, g, kx, held,
            )
            ends.append(b)
        return ends, (b, g, low, high)

    base = lax.dynamic_index_in_dim(held, scal[4], 0, False)
    early_ends, _ = chain(base, 1, HALF - 1)
    late_start = move(early_ends[-1], route(lambda t, s: (t ^ HALF, s)))
    late_ends, (cb, cg, clow, chigh) = chain(late_start, 0, HALF - 1)

    b, g, low, high = call(
        again_kernel, BEGUN, [ROWS], scal, *fine, anchor, forces, *early_ends, *late_ends
    )
    ckx = cross(coarse_faces, clow, chigh)
    kx = cross(fine_faces, low, high)
    below, above = exchange(jnp.concatenate([low, clow]), jnp.concatenate([high, chigh]))
    v1, b, g, low, high = call(
        functools.partial(fine_kernel, 1), [STATE, *BEGUN], [ROWS],
        scal, *fine, below, above, b, g, kx, forces,
    )
    (last_end,) = call(
        functools.partial(turn_kernel, HALF - 1, 2 * TRACE, False), [STATE], [ROWS],
        scal, *coarse, below, above, cb, cg, ckx, held,
    )
    v2, b, g, low, high = fine_step(2, b, g, low, high)
    kx = cross(fine_faces, low, high)
    below, above = exchange(low, high)
    (out,) = call(
        last_kernel, [((4, DOFS, ELEMS), F32)], [ROWS],
        scal, *fine, below, above, b, g, kx, ends, back, v1, v2, *early_ends, *late_ends, last_end,
        hbm_out=True,
    )
    return out


def solution(mesh):
    in_specs = (
        P(None, "space"),
        P("tm", None, "space"),
        P("tm", None, "space"),
        P(None, None, "space"),
        P(None, None, "space"),
        P(None, "space"),
        P("space"),
        P("space"),
        P(),
        P(),
    )
    out_specs = P("tm", None, "space")
    return jax.shard_map(local, mesh=mesh, in_specs=in_specs, out_specs=out_specs, check_vma=False)
```

```python
import functools

import jax
import jax.numpy as jnp
from jax import lax
from jax.experimental import pallas as pl
from jax.experimental.pallas import tpu as pltpu
from jax.sharding import PartitionSpec as P

DOFS = 64
TRACE = 32
LANES = 128
ELEMS = 256
HALF = 8
PARTS = 4
F32 = jnp.float32
BF16 = jnp.bfloat16

VMEM = pl.BlockSpec(memory_space=pltpu.VMEM)
SMEM = pl.BlockSpec(memory_space=pltpu.SMEM)
ANY = pl.BlockSpec(memory_space=pl.ANY)


class Stream:
    def __init__(self, source, target, sems):
        self.target, self.copies = target, []
        for c in range(PARTS):
            rows = pl.ds(c * (DOFS // PARTS), DOFS // PARTS)
            self.copies.append(pltpu.make_async_copy(source.at[rows], target.at[rows], sems.at[c]))
            self.copies[-1].start()

    def ready(self):
        for copy in self.copies:
            copy.wait()
        self.copies = []
        return self.target


def halves(x):
    high = x.astype(BF16)
    return high, (x - high.astype(F32)).astype(BF16)


def dot(a, b):
    return jnp.dot(a, b, preferred_element_type=F32)


def dot3(weights, x):
    high, low = halves(x)
    return dot(weights, jnp.concatenate([high, low, high], axis=0))


def split_weights(w):
    high, low = halves(w)
    return jnp.concatenate([high.astype(F32), high.astype(F32), low.astype(F32)], axis=1).astype(BF16)


def pick(source, lane):
    lane = jnp.broadcast_to(lane, source.shape)
    return jnp.take_along_axis(source, lane, axis=1, mode="promise_in_bounds")


def pick_wide(source, index):
    lane = index & (LANES - 1)
    first, second = pick(source[:, :LANES], lane), pick(source[:, LANES:], lane)
    return jnp.where(jnp.broadcast_to(index, first.shape) < LANES, first, second)


def reorder(source, first_ref, second_ref):
    return jnp.concatenate([pick_wide(source, first_ref[...]), pick_wide(source, second_ref[...])], axis=1)


def gathered(traces, below, above, near_ref):
    nothing = jnp.zeros((TRACE, LANES), F32)
    rows = []
    for face in range(6):
        first = (face ^ 1) * TRACE
        low = traces[first : first + TRACE, :LANES]
        high = traces[first : first + TRACE, LANES:]
        if face == 0:
            pair = [nothing if below is None else below, pick(low, near_ref[0:1, :])]
        elif face == 1:
            pair = [pick(high, near_ref[1:2, :]), nothing if above is None else above]
        else:
            pair = [pick(low, near_ref[2 * face - 2 : 2 * face - 1, :]), pick(high, near_ref[2 * face - 1 : 2 * face, :])]
        rows.append(jnp.concatenate(pair, axis=1))
    return jnp.concatenate(rows, axis=0)


def apply_inverse(q_ref, d_ref, rows_ref, right):
    rows_ref[...] = right
    if isinstance(q_ref, Stream):
        q_ref = q_ref.ready()

    def step(chunk, total):
        for k in range(8):
            j = chunk * 8 + k
            total = total - q_ref[j] * rows_ref[pl.ds(j, 1), :]
        return total

    return lax.fori_loop(0, DOFS // 8, step, 2.0 * d_ref[...] * right)


def apply_edges(low_ref, high_ref, rows_ref, below, above, start):
    rows_ref[:TRACE, :LANES] = below
    rows_ref[:TRACE, LANES:] = above

    def step(chunk, total):
        low, high = total
        tile = rows_ref[pl.ds(pl.multiple_of(chunk * 8, 8), 8), :]
        for k in range(8):
            u = chunk * 8 + k
            block = pl.ds(pl.multiple_of(u * DOFS, DOFS), DOFS)
            low = low - low_ref[block, :] * tile[k : k + 1, :LANES]
            high = high - high_ref[block, :] * tile[k : k + 1, LANES:]
        return low, high

    total = lax.fori_loop(0, TRACE // 8, step, (start[:, :LANES], start[:, LANES:]))
    return jnp.concatenate(total, axis=1)


def tables_kernel(trace_ref, lift_ref, nbr_ref, slow_ref, shigh_ref, wt_ref, wl_ref, near_ref, back0_ref, back1_ref):
    wt_ref[...] = split_weights(trace_ref[...])
    wl_ref[...] = split_weights(lift_ref[...])
    sends = (slow_ref, shigh_ref)
    position = lax.broadcasted_iota(jnp.int32, (LANES, LANES), 0)
    lane = lax.broadcasted_iota(jnp.int32, (LANES, LANES), 1)
    places = []
    for half in range(2):
        place = jnp.zeros((1, LANES), F32)
        for layer in range(2):
            ids = jnp.broadcast_to(sends[layer][...], (LANES, LANES)).astype(F32)
            ids = jnp.transpose(ids).astype(jnp.int32)
            here = jnp.where(ids == lane + half * LANES, position + layer * LANES, 0).astype(F32)
            place = place + jnp.sum(here, axis=0, keepdims=True)
        places.append(place.astype(jnp.int32))
    back0_ref[...] = places[0]
    back1_ref[...] = places[1]
    place = jnp.broadcast_to(jnp.concatenate(places, axis=1), (8, ELEMS))
    order = [(0, 1), (1, 0)] + [(face, layer) for face in range(2, 6) for layer in range(2)]
    for row, (face, layer) in enumerate(order):
        ids = pick_wide(jnp.broadcast_to(nbr_ref[face : face + 1, :], (8, ELEMS)), sends[layer][...])
        near_ref[row : row + 1, :] = (pick_wide(place, ids[0:1]) & (LANES - 1))[0:1]


def prepare_kernel(scal_ref, q_ref, slow_ref, shigh_ref, trace_ref, lift_ref,
                   out_ref, d_ref, rlow_ref, rhigh_ref, klow_ref, khigh_ref, held_ref, sems, out_sems):
    def fetch(c):
        rows = pl.ds(c * 8, 8)
        return pltpu.make_async_copy(q_ref.at[rows], held_ref.at[rows], sems.at[c])

    def put(c):
        rows = pl.ds(c * 8, 8)
        return pltpu.make_async_copy(held_ref.at[rows], out_ref.at[rows], out_sems.at[c])

    for c in range(DOFS // 8):
        fetch(c).start()
    lift = split_weights(lift_ref[: 2 * TRACE, :])
    tr = split_weights(trace_ref[: 2 * TRACE, :])

    def chunk(c, carry):
        fetch(c).wait()
        for k in range(8):
            i = c * 8 + k
            q = reorder(held_ref[i], slow_ref, shigh_ref)
            held_ref[i] = q
            d_ref[pl.ds(i, 1), :] = held_ref[i, pl.ds(i, 1), :]
            r = dot3(lift, q)
            place = pl.ds(i, TRACE, stride=DOFS)
            rlow_ref[place, :] = r[:TRACE, :LANES]
            rhigh_ref[place, :] = r[TRACE:, LANES:]
        put(c).start()
        return carry

    lax.fori_loop(0, DOFS // 8, chunk, 0)
    first = scal_ref[4] * (TRACE // 2)

    def faces(c, carry):
        for k in range(4):
            n = c * 4 + k
            rows = pl.ds(pl.multiple_of((first + n) * DOFS, DOFS), DOFS)
            made = dot3(tr, jnp.concatenate([rlow_ref[rows, :], rhigh_ref[rows, :]], axis=1))
            place = pl.ds(pl.multiple_of(n * TRACE, TRACE), TRACE)
            klow_ref[place, :] = made[:TRACE, :LANES]
            khigh_ref[place, :] = made[TRACE:, LANES:]
        return carry

    lax.fori_loop(0, TRACE // 8, faces, 0)
    for c in range(DOFS // 8):
        put(c).wait()


def reorder_kernel(force_ref, guess_ref, slow_ref, shigh_ref, force_out_ref, guess_out_ref):
    for step in range(4):
        force_out_ref[step] = reorder(force_ref[step], slow_ref, shigh_ref)
    guess_out_ref[...] = reorder(guess_ref[...], slow_ref, shigh_ref)


def finish(scal_ref, w, below_ref, above_ref, first, u_ref, b_ref, kx_ref, rows_ref):
    q_ref, rlow_ref, rhigh_ref, d_ref, near_ref, wt_ref, wl_ref = w
    below = jnp.where(scal_ref[0] == 1, below_ref[first : first + 2 * TRACE, :], 0.0)
    above = jnp.where(scal_ref[1] == 1, above_ref[first : first + 2 * TRACE, :], 0.0)
    v1 = apply_edges(rlow_ref, rhigh_ref, rows_ref, below[TRACE:], above[TRACE:], u_ref[...])
    traces = dot3(wt_ref[...], v1)
    below = below[:TRACE] - kx_ref[:TRACE, :]
    above = above[:TRACE] - kx_ref[TRACE:, :]
    coupled = dot3(wl_ref[...], gathered(traces, below, above, near_ref))
    return apply_inverse(q_ref, d_ref, rows_ref, b_ref[...] - coupled)


def begin(w, v, b, outs, rows_ref):
    q_ref, rlow_ref, rhigh_ref, d_ref, near_ref, wt_ref, wl_ref = w
    b_ref, u_ref, low_ref, high_ref = outs
    traces = dot3(wt_ref[...], v)
    coupled = dot3(wl_ref[...], gathered(traces, None, None, near_ref))
    u = apply_inverse(q_ref, d_ref, rows_ref, b - coupled)
    ends = dot3(wt_ref[: 2 * TRACE, :], u)
    b_ref[...] = b
    u_ref[...] = u
    low_ref[:TRACE, :] = ends[:TRACE, :LANES]
    low_ref[TRACE:, :] = traces[:TRACE, :LANES]
    high_ref[:TRACE, :] = ends[TRACE:, LANES:]
    high_ref[TRACE:, :] = traces[TRACE : 2 * TRACE, LANES:]


def cross_kernel(scal_ref, kb0_ref, ka0_ref, kb1_ref, ka1_ref, low_ref, high_ref, kx_ref, rows_ref):
    rows_ref[:, :LANES] = low_ref[TRACE:, :]
    rows_ref[:, LANES:] = high_ref[TRACE:, :]
    half = TRACE // 2

    def step(chunk, total):
        below, above = total
        for kb_ref, ka_ref, core in ((kb0_ref, ka0_ref, scal_ref[4]), (kb1_ref, ka1_ref, 1 - scal_ref[4])):
            tile = rows_ref[pl.ds(pl.multiple_of(core * half + chunk * 8, 8), 8), :]
            for k in range(8):
                place = pl.ds(pl.multiple_of((chunk * 8 + k) * TRACE, TRACE), TRACE)
                below = below + kb_ref[place, :] * tile[k : k + 1, :LANES]
                above = above + ka_ref[place, :] * tile[k : k + 1, LANES:]
        return below, above

    nothing = jnp.zeros((TRACE, LANES), F32)
    below, above = lax.fori_loop(0, half // 8, step, (nothing, nothing))
    kx_ref[:TRACE, :] = jnp.where(scal_ref[0] == 1, below, 0.0)
    kx_ref[TRACE:, :] = jnp.where(scal_ref[1] == 1, above, 0.0)


def first_kernel(q_ref, rlow_ref, rhigh_ref, d_ref, near_ref, wt_ref, wl_ref, anchor_ref, slow_ref, shigh_ref, force_ref, v_ref, *outs):
    v = reorder(anchor_ref[...], slow_ref, shigh_ref)
    v_ref[...] = v
    begin((q_ref, rlow_ref, rhigh_ref, d_ref, near_ref, wt_ref, wl_ref), v, v + force_ref[0], outs[:4], outs[4])


def again_kernel(scal_ref, q_ref, rlow_ref, rhigh_ref, d_ref, near_ref, wt_ref, wl_ref, anchor_ref, force_ref, *refs):
    ends, outs = refs[:-5], refs[-5:]
    turn = scal_ref[2]
    before = jnp.zeros((DOFS, ELEMS), F32)
    for k, end_ref in enumerate(ends):
        before = jnp.where(turn == k, end_ref[...], before)
    v = anchor_ref[...] + before
    begin((q_ref, rlow_ref, rhigh_ref, d_ref, near_ref, wt_ref, wl_ref), v, v + force_ref[0], outs[:4], outs[4])


def fine_kernel(step, keep, scal_ref, q_ref, rlow_ref, rhigh_ref, d_ref, near_ref, wt_ref, wl_ref,
                below_ref, above_ref, bin_ref, uin_ref, kx_ref, force_ref, *outs):
    w = (q_ref, rlow_ref, rhigh_ref, d_ref, near_ref, wt_ref, wl_ref)
    v = finish(scal_ref, w, below_ref, above_ref, 0, uin_ref, bin_ref, kx_ref, outs[-1])
    begin(w, v, v + force_ref[step], outs[:4], outs[-1])
    if keep:
        outs[4][...] = v


def residual_kernel(scal_ref, q_ref, rlow_ref, rhigh_ref, d_ref, near_ref, wt_ref, wl_ref,
                    below_ref, above_ref, bin_ref, uin_ref, kx_ref, guess_ref, v_ref, rows_ref):
    w = (q_ref, rlow_ref, rhigh_ref, d_ref, near_ref, wt_ref, wl_ref)
    v = finish(scal_ref, w, below_ref, above_ref, 0, uin_ref, bin_ref, kx_ref, rows_ref)
    v_ref[...] = v - guess_ref[...]


def last_kernel(scal_ref, q_ref, rlow_ref, rhigh_ref, d_ref, near_ref, wt_ref, wl_ref,
                below_ref, above_ref, bin_ref, uin_ref, kx_ref, guess_ref, back0_ref, back1_ref, v1_ref, v2_ref, *refs):
    ends, (out_ref, rows_ref) = refs[:-2], refs[-2:]
    w = (q_ref, rlow_ref, rhigh_ref, d_ref, near_ref, wt_ref, wl_ref)
    v = finish(scal_ref, w, below_ref, above_ref, 0, uin_ref, bin_ref, kx_ref, rows_ref)
    out_ref[0] = reorder(v1_ref[...], back0_ref, back1_ref)
    out_ref[1] = reorder(v2_ref[...], back0_ref, back1_ref)
    out_ref[2] = reorder(v, back0_ref, back1_ref)
    turn = scal_ref[3]
    after = jnp.zeros((DOFS, ELEMS), F32)
    for k, end_ref in enumerate(ends):
        after = jnp.where(turn == k, end_ref[...], after)
    out_ref[3] = reorder(guess_ref[...] + after, back0_ref, back1_ref)


def start_kernel(q_ref, rlow_ref, rhigh_ref, d_ref, near_ref, wt_ref, wl_ref, v_ref, *outs):
    v = v_ref[...]
    begin((q_ref, rlow_ref, rhigh_ref, d_ref, near_ref, wt_ref, wl_ref), v, v, outs[:4], outs[4])


def turn_kernel(turn, first, more, scal_ref, q_ref, rlow_ref, rhigh_ref, d_ref, near_ref, wt_ref, wl_ref,
                below_ref, above_ref, bin_ref, uin_ref, kx_ref, res_ref, *outs):
    w = (q_ref, rlow_ref, rhigh_ref, d_ref, near_ref, wt_ref, wl_ref)
    v = finish(scal_ref, w, below_ref, above_ref, first, uin_ref, bin_ref, kx_ref, outs[-1])
    v = v + res_ref[scal_ref[5 + turn]]
    if more:
        begin(w, v, v, outs[:4], outs[4])
    else:
        outs[0][...] = v


STATE = ((DOFS, ELEMS), F32)
EDGE = ((2 * TRACE, LANES), F32)
FACES = ((TRACE // 2 * TRACE, LANES), F32)
EDGES = ((TRACE * DOFS, LANES), F32)
INVERSE = ((DOFS, DOFS, ELEMS), F32)
ROWS = pltpu.VMEM((DOFS, ELEMS), F32)
FACE_ROWS = pltpu.VMEM((TRACE, ELEMS), F32)
BEGUN = (STATE, STATE, EDGE, EDGE)
VMEM_LIMIT = 4 << 20


def near_by(x):
    return pltpu.with_memory_space_constraint(x, pltpu.VMEM)


def far_off(x):
    return pltpu.with_memory_space_constraint(x, pltpu.HBM)


def call(kernel, outs, scratch, *args, scalars=True, hbm_in=(), hbm_out=(), windows=(), limit=VMEM_LIMIT, busy=None):
    specs = [VMEM] * len(args)
    if scalars:
        specs[0] = SMEM
    for n in hbm_in:
        specs[n] = ANY
    return pl.pallas_call(
        kernel,
        out_shape=[(pltpu.HBM if n in (*hbm_out, *windows) else pltpu.VMEM)(*x) for n, x in enumerate(outs)],
        in_specs=specs,
        out_specs=[ANY if n in hbm_out else VMEM for n in range(len(outs))],
        scratch_shapes=scratch,
        compiler_params=pltpu.CompilerParams(vmem_limit_bytes=limit),
        cost_estimate=None if busy is None else pl.CostEstimate(flops=0, bytes_accessed=busy, transcendentals=0),
    )(*args)


class Operator:
    def __init__(self, inverse, rest, stream):
        self.inverse, self.rest, self.stream = inverse, rest, stream

    def call(self, kernel, outs, *args, scal=None, final=False, far=()):
        lead = [] if scal is None else [scal]
        fixed = [self.inverse, *self.rest]
        place, stream = len(lead), self.stream
        args = lead + fixed + list(args)
        specs = [SMEM] * place + [VMEM] * (len(args) - place)
        for n in range(place, len(args)):
            if n == place and stream:
                args[n] = far_off(args[n])
                specs[n] = ANY
            elif n - place - len(fixed) not in far:
                args[n] = near_by(args[n])

        def body(*refs):
            refs = list(refs)
            if stream:
                refs, (target, sems) = refs[:-2], refs[-2:]
                refs[place] = Stream(refs[place], target, sems)
            kernel(*refs)

        kind = jax.ShapeDtypeStruct if final else pltpu.VMEM
        fetch = [pltpu.VMEM((DOFS, DOFS, ELEMS), F32), pltpu.SemaphoreType.DMA((PARTS,))] if stream else []
        return pl.pallas_call(
            body,
            out_shape=[kind(*x) for x in outs],
            in_specs=specs,
            out_specs=[VMEM] * len(outs),
            scratch_shapes=[ROWS] + fetch,
            compiler_params=pltpu.CompilerParams(vmem_limit_bytes=(8 << 20) if stream else VMEM_LIMIT),
        )(*args)


def local(
    initial,
    guess,
    forcing,
    fine_inverse,
    coarse_inverse,
    neighbour,
    send_low,
    send_high,
    trace_map,
    lift_map,
):
    times = lax.axis_size("tm")
    blocks = lax.axis_size("space")
    now = lax.axis_index("tm")
    place = lax.axis_index("space")
    guess = guess[0]

    def route(target):
        return [
            (t * blocks + s, a * blocks + b)
            for t in range(times)
            for s in range(blocks)
            for a, b in [target(t, s)]
        ]

    def shift(by, across=0):
        def target(t, s):
            there = s + by
            if 0 <= there < blocks:
                return (t + across) % times, there
            return (t + HALF - across) % times, there % blocks

        return route(target)

    up, down = shift(1), shift(-1)
    swap_cores = route(lambda t, s: (t ^ 1, s))
    swap_halves = route(lambda t, s: (t ^ HALF, s))

    def move(x, pairs):
        return lax.ppermute(x, ("tm", "space"), pairs)

    def exchange(low, high, up=up, down=down):
        above = move(low, down)
        below = move(high, up)
        return below, above

    group, core = now % HALF // 2, now % 2
    turns = jnp.arange(HALF)
    slots = (group - turns // 2) % 4 + 4 * (turns % 2 ^ core)
    early = now < HALF
    turn = now % HALF
    before = jnp.where(early, turn - 1, HALF + turn)
    after = jnp.where(early, turn, HALF + turn + 1)
    scal = jnp.concatenate([jnp.stack([place > 0, place < blocks - 1, before, after, core]), slots]).astype(jnp.int32)

    slow, shigh = send_low.reshape(1, LANES), send_high.reshape(1, LANES)
    traces = trace_map.reshape(6 * TRACE, DOFS)
    lifts = jnp.transpose(lift_map, (0, 2, 1)).reshape(6 * TRACE, DOFS)
    ahead = [(i, i + 1) for i in range(times - 1)]
    moved = lax.ppermute(guess, "tm", ahead)

    def prepare(inverse, scal, windows=()):
        q, d, rlow, rhigh, klow, khigh = call(
            prepare_kernel,
            [INVERSE, STATE, EDGES, EDGES, FACES, FACES],
            [pltpu.VMEM((DOFS, DOFS, ELEMS), F32)] + [pltpu.SemaphoreType.DMA((DOFS // 8,))] * 2,
            scal, *map(far_off, (inverse, slow, shigh, traces, lifts)),
            hbm_in=(1,), hbm_out=(0,), windows=windows, limit=10 << 20, busy=24 << 20,
        )
        return q, (rlow, rhigh, d), (klow, khigh)

    def both_halves(faces):
        return (*faces, *[move(x, swap_cores) for x in faces])

    def cross(faces, low, high):
        args = [near_by(x) for x in (*faces, low, high)]
        (kx,) = call(cross_kernel, [EDGE], [FACE_ROWS], scal, *args, busy=2 << 20)
        return kx

    fine_inverse, fine_rest, fine_faces = prepare(fine_inverse, scal)
    fine_faces = exchange(*fine_faces)
    wt, wl, near, back0, back1 = call(
        tables_kernel,
        [((192, 192), BF16), ((64, 576), BF16), ((16, LANES), jnp.int32), ((1, LANES), jnp.int32), ((1, LANES), jnp.int32)],
        [],
        *map(far_off, (traces, jnp.transpose(lift_map, (1, 0, 2)).reshape(DOFS, 6 * TRACE), neighbour, slow, shigh)),
        scalars=False,
    )
    forces, goal = call(
        reorder_kernel, [((4, DOFS, ELEMS), F32), STATE], [], *map(far_off, (forcing, guess, slow, shigh)), scalars=False
    )
    fine = Operator(fine_inverse, (*fine_rest, near, wt, wl), False)
    start = jnp.where(now == 0, initial, moved)
    anchor, b, u, low, high = fine.call(
        first_kernel, [STATE, *BEGUN], start, far_off(slow), far_off(shigh), forces, far=(0, 1, 2)
    )
    low, later = lax.optimization_barrier((low, scal))
    coarse_inverse, coarse_rest, coarse_faces = prepare(coarse_inverse, later, (2, 3))
    coarse = Operator(coarse_inverse, (*coarse_rest, near, wt, wl), False)
    fine_faces = both_halves(lax.optimization_barrier((*fine_faces, coarse_rest[2]))[:2])

    def fine_step(step, keep, b, u, low, high):
        kx = cross(fine_faces, low, high)
        below, above = exchange(low, high)
        return fine.call(
            functools.partial(fine_kernel, step, keep), [*BEGUN, STATE] if keep else BEGUN,
            below, above, b, u, kx, forces, scal=scal,
        )

    for step in (1, 2, 3):
        b, u, low, high = fine_step(step, False, b, u, low, high)
    kx = cross(fine_faces, low, high)
    below, above = exchange(low, high)
    (residual,) = fine.call(residual_kernel, [STATE], below, above, b, u, kx, goal, scal=scal)

    residual, *coarse_faces = lax.optimization_barrier((residual, *coarse_faces))
    coarse_faces = both_halves(exchange(*coarse_faces))

    def turned(k):
        return route(lambda t, s: (t // HALF * HALF + (t % HALF + 2 * k) % HALF, s))

    held = jnp.stack([residual] + [move(residual, turned(k)) for k in (1, 2, 3)])
    held = jnp.concatenate([held, move(held, swap_cores)])

    def chain(first, count, b, u, low, high, edges=None):
        ends = []
        for turn in range(first, first + count):
            kx = cross(coarse_faces, low, high)
            below, above = exchange(low, high) if edges is None else edges
            edges = None
            b, u, low, high = coarse.call(
                functools.partial(turn_kernel, turn, 0, True), BEGUN, below, above, b, u, kx, held, scal=scal
            )
            ends.append(b)
        return ends, (b, u, low, high)

    base = lax.dynamic_index_in_dim(held, scal[5], 0, False)
    early_ends, (b, u, low, high) = chain(1, HALF - 1, *coarse.call(start_kernel, BEGUN, base))
    early_ends = [base] + early_ends
    edges = exchange(low, high, shift(1, HALF), shift(-1, HALF))
    late_start = move(b, swap_halves)
    late_ends, (cb, cu, clow, chigh) = chain(0, HALF - 1, *coarse.call(start_kernel, BEGUN, late_start), edges)
    late_ends = [late_start] + late_ends

    b, u, low, high = fine.call(again_kernel, BEGUN, anchor, forces, *early_ends, *late_ends, scal=scal)
    ckx = cross(coarse_faces, clow, chigh)
    kx = cross(fine_faces, low, high)
    below, above = exchange(jnp.concatenate([low, clow]), jnp.concatenate([high, chigh]))
    b, u, low, high, v1 = fine.call(
        functools.partial(fine_kernel, 1, True), [*BEGUN, STATE], below, above, b, u, kx, forces, scal=scal
    )
    (last_end,) = coarse.call(
        functools.partial(turn_kernel, HALF - 1, 2 * TRACE, False), [STATE], below, above, cb, cu, ckx, held, scal=scal
    )
    b, u, low, high, v2 = fine_step(2, True, b, u, low, high)
    kx = cross(fine_faces, low, high)
    below, above = exchange(low, high)
    (out,) = fine.call(
        last_kernel, [((4, DOFS, ELEMS), F32)],
        below, above, b, u, kx, goal, back0, back1, v1, v2, *early_ends, *late_ends, last_end,
        scal=scal, final=True,
    )
    return out


def solution(mesh):
    in_specs = (
        P(None, "space"),
        P("tm", None, "space"),
        P("tm", None, "space"),
        P(None, None, "space"),
        P(None, None, "space"),
        P(None, "space"),
        P("space"),
        P("space"),
        P(),
        P(),
    )
    out_specs = P("tm", None, "space")
    return jax.shard_map(local, mesh=mesh, in_specs=in_specs, out_specs=out_specs, check_vma=False)
```

```python
import functools

import jax
import jax.numpy as jnp
from jax import lax
from jax.experimental import pallas as pl
from jax.experimental.pallas import tpu as pltpu
from jax.sharding import PartitionSpec as P

DOFS = 64
TRACE = 32
LANES = 128
ELEMS = 256
HALF = 8
PARTS = 4
F32 = jnp.float32
BF16 = jnp.bfloat16

VMEM = pl.BlockSpec(memory_space=pltpu.VMEM)
SMEM = pl.BlockSpec(memory_space=pltpu.SMEM)
ANY = pl.BlockSpec(memory_space=pl.ANY)


class Stream:
    def __init__(self, source, target, sems):
        self.target, self.copies = target, []
        for c in range(PARTS):
            rows = pl.ds(c * (DOFS // PARTS), DOFS // PARTS)
            self.copies.append(pltpu.make_async_copy(source.at[rows], target.at[rows], sems.at[c]))
            self.copies[-1].start()

    def ready(self):
        for copy in self.copies:
            copy.wait()
        self.copies = []
        return self.target


def halves(x):
    high = x.astype(BF16)
    return high, (x - high.astype(F32)).astype(BF16)


def dot(a, b):
    return jnp.dot(a, b, preferred_element_type=F32)


def dot3(weights, x):
    high, low = halves(x)
    return dot(weights, jnp.concatenate([high, low, high], axis=0))


def split_weights(w):
    high, low = halves(w)
    return jnp.concatenate([high.astype(F32), high.astype(F32), low.astype(F32)], axis=1).astype(BF16)


def pick(source, lane):
    lane = jnp.broadcast_to(lane, source.shape)
    return jnp.take_along_axis(source, lane, axis=1, mode="promise_in_bounds")


def pick_wide(source, index):
    lane = index & (LANES - 1)
    first, second = pick(source[:, :LANES], lane), pick(source[:, LANES:], lane)
    return jnp.where(jnp.broadcast_to(index, first.shape) < LANES, first, second)


def reorder(source, first_ref, second_ref):
    return jnp.concatenate([pick_wide(source, first_ref[...]), pick_wide(source, second_ref[...])], axis=1)


def gathered(traces, below, above, near_ref):
    nothing = jnp.zeros((TRACE, LANES), F32)
    rows = []
    for face in range(6):
        first = (face ^ 1) * TRACE
        low = traces[first : first + TRACE, :LANES]
        high = traces[first : first + TRACE, LANES:]
        if face == 0:
            pair = [nothing if below is None else below, pick(low, near_ref[0:1, :])]
        elif face == 1:
            pair = [pick(high, near_ref[1:2, :]), nothing if above is None else above]
        else:
            pair = [pick(low, near_ref[2 * face - 2 : 2 * face - 1, :]), pick(high, near_ref[2 * face - 1 : 2 * face, :])]
        rows.append(jnp.concatenate(pair, axis=1))
    return jnp.concatenate(rows, axis=0)


def apply_inverse(q_ref, d_ref, rows_ref, right):
    rows_ref[...] = right
    if isinstance(q_ref, Stream):
        q_ref = q_ref.ready()

    def step(chunk, total):
        for k in range(8):
            j = chunk * 8 + k
            total = total - q_ref[j] * rows_ref[pl.ds(j, 1), :]
        return total

    return lax.fori_loop(0, DOFS // 8, step, 2.0 * d_ref[...] * right)


def apply_edges(low_ref, high_ref, rows_ref, below, above, start):
    rows_ref[:TRACE, :LANES] = below
    rows_ref[:TRACE, LANES:] = above

    def step(chunk, total):
        low, high = total
        tile = rows_ref[pl.ds(pl.multiple_of(chunk * 8, 8), 8), :]
        for k in range(8):
            u = chunk * 8 + k
            block = pl.ds(pl.multiple_of(u * DOFS, DOFS), DOFS)
            low = low - low_ref[block, :] * tile[k : k + 1, :LANES]
            high = high - high_ref[block, :] * tile[k : k + 1, LANES:]
        return low, high

    total = lax.fori_loop(0, TRACE // 8, step, (start[:, :LANES], start[:, LANES:]))
    return jnp.concatenate(total, axis=1)


def tables_kernel(trace_ref, lift_ref, nbr_ref, slow_ref, shigh_ref, wt_ref, wl_ref, near_ref, back0_ref, back1_ref):
    wt_ref[...] = split_weights(trace_ref[...])
    wl_ref[...] = split_weights(lift_ref[...])
    sends = (slow_ref, shigh_ref)
    position = lax.broadcasted_iota(jnp.int32, (LANES, LANES), 0)
    lane = lax.broadcasted_iota(jnp.int32, (LANES, LANES), 1)
    places = []
    for half in range(2):
        place = jnp.zeros((1, LANES), F32)
        for layer in range(2):
            ids = jnp.broadcast_to(sends[layer][...], (LANES, LANES)).astype(F32)
            ids = jnp.transpose(ids).astype(jnp.int32)
            here = jnp.where(ids == lane + half * LANES, position + layer * LANES, 0).astype(F32)
            place = place + jnp.sum(here, axis=0, keepdims=True)
        places.append(place.astype(jnp.int32))
    back0_ref[...] = places[0]
    back1_ref[...] = places[1]
    place = jnp.broadcast_to(jnp.concatenate(places, axis=1), (8, ELEMS))
    order = [(0, 1), (1, 0)] + [(face, layer) for face in range(2, 6) for layer in range(2)]
    for row, (face, layer) in enumerate(order):
        ids = pick_wide(jnp.broadcast_to(nbr_ref[face : face + 1, :], (8, ELEMS)), sends[layer][...])
        near_ref[row : row + 1, :] = (pick_wide(place, ids[0:1]) & (LANES - 1))[0:1]


def prepare_kernel(scal_ref, q_ref, slow_ref, shigh_ref, trace_ref, lift_ref,
                   out_ref, d_ref, rlow_ref, rhigh_ref, klow_ref, khigh_ref, held_ref, sems, out_sems):
    def fetch(c):
        rows = pl.ds(c * 8, 8)
        return pltpu.make_async_copy(q_ref.at[rows], held_ref.at[rows], sems.at[c])

    def put(c):
        rows = pl.ds(c * 8, 8)
        return pltpu.make_async_copy(held_ref.at[rows], out_ref.at[rows], out_sems.at[c])

    for c in range(DOFS // 8):
        fetch(c).start()
    lift = split_weights(lift_ref[: 2 * TRACE, :])
    tr = split_weights(trace_ref[: 2 * TRACE, :])

    def chunk(c, carry):
        fetch(c).wait()
        for k in range(8):
            i = c * 8 + k
            q = reorder(held_ref[i], slow_ref, shigh_ref)
            held_ref[i] = q
            d_ref[pl.ds(i, 1), :] = held_ref[i, pl.ds(i, 1), :]
            r = dot3(lift, q)
            place = pl.ds(i, TRACE, stride=DOFS)
            rlow_ref[place, :] = r[:TRACE, :LANES]
            rhigh_ref[place, :] = r[TRACE:, LANES:]
        put(c).start()
        return carry

    lax.fori_loop(0, DOFS // 8, chunk, 0)
    first = scal_ref[4] * (TRACE // 2)

    def faces(c, carry):
        for k in range(4):
            n = c * 4 + k
            rows = pl.ds(pl.multiple_of((first + n) * DOFS, DOFS), DOFS)
            made = dot3(tr, jnp.concatenate([rlow_ref[rows, :], rhigh_ref[rows, :]], axis=1))
            place = pl.ds(pl.multiple_of(n * TRACE, TRACE), TRACE)
            klow_ref[place, :] = made[:TRACE, :LANES]
            khigh_ref[place, :] = made[TRACE:, LANES:]
        return carry

    lax.fori_loop(0, TRACE // 8, faces, 0)
    for c in range(DOFS // 8):
        put(c).wait()


def reorder_kernel(force_ref, guess_ref, slow_ref, shigh_ref, force_out_ref, guess_out_ref):
    for step in range(4):
        force_out_ref[step] = reorder(force_ref[step], slow_ref, shigh_ref)
    guess_out_ref[...] = reorder(guess_ref[...], slow_ref, shigh_ref)


def finish(scal_ref, w, below_ref, above_ref, first, u_ref, b_ref, kx_ref, rows_ref):
    q_ref, rlow_ref, rhigh_ref, d_ref, near_ref, wt_ref, wl_ref = w
    below = jnp.where(scal_ref[0] == 1, below_ref[first : first + 2 * TRACE, :], 0.0)
    above = jnp.where(scal_ref[1] == 1, above_ref[first : first + 2 * TRACE, :], 0.0)
    v1 = apply_edges(rlow_ref, rhigh_ref, rows_ref, below[TRACE:], above[TRACE:], u_ref[...])
    traces = dot3(wt_ref[...], v1)
    below = below[:TRACE] - kx_ref[:TRACE, :]
    above = above[:TRACE] - kx_ref[TRACE:, :]
    coupled = dot3(wl_ref[...], gathered(traces, below, above, near_ref))
    return apply_inverse(q_ref, d_ref, rows_ref, b_ref[...] - coupled)


def begin(w, v, b, outs, rows_ref):
    q_ref, rlow_ref, rhigh_ref, d_ref, near_ref, wt_ref, wl_ref = w
    b_ref, u_ref, low_ref, high_ref = outs
    traces = dot3(wt_ref[...], v)
    coupled = dot3(wl_ref[...], gathered(traces, None, None, near_ref))
    u = apply_inverse(q_ref, d_ref, rows_ref, b - coupled)
    ends = dot3(wt_ref[: 2 * TRACE, :], u)
    b_ref[...] = b
    u_ref[...] = u
    low_ref[:TRACE, :] = ends[:TRACE, :LANES]
    low_ref[TRACE:, :] = traces[:TRACE, :LANES]
    high_ref[:TRACE, :] = ends[TRACE:, LANES:]
    high_ref[TRACE:, :] = traces[TRACE : 2 * TRACE, LANES:]


def cross_kernel(scal_ref, kb0_ref, ka0_ref, kb1_ref, ka1_ref, low_ref, high_ref, kx_ref, rows_ref):
    rows_ref[:, :LANES] = low_ref[TRACE:, :]
    rows_ref[:, LANES:] = high_ref[TRACE:, :]
    half = TRACE // 2

    def step(chunk, total):
        below, above = total
        for kb_ref, ka_ref, core in ((kb0_ref, ka0_ref, scal_ref[4]), (kb1_ref, ka1_ref, 1 - scal_ref[4])):
            tile = rows_ref[pl.ds(pl.multiple_of(core * half + chunk * 8, 8), 8), :]
            for k in range(8):
                place = pl.ds(pl.multiple_of((chunk * 8 + k) * TRACE, TRACE), TRACE)
                below = below + kb_ref[place, :] * tile[k : k + 1, :LANES]
                above = above + ka_ref[place, :] * tile[k : k + 1, LANES:]
        return below, above

    nothing = jnp.zeros((TRACE, LANES), F32)
    below, above = lax.fori_loop(0, half // 8, step, (nothing, nothing))
    kx_ref[:TRACE, :] = jnp.where(scal_ref[0] == 1, below, 0.0)
    kx_ref[TRACE:, :] = jnp.where(scal_ref[1] == 1, above, 0.0)


def first_kernel(q_ref, rlow_ref, rhigh_ref, d_ref, near_ref, wt_ref, wl_ref, anchor_ref, slow_ref, shigh_ref, force_ref, v_ref, *outs):
    v = reorder(anchor_ref[...], slow_ref, shigh_ref)
    v_ref[...] = v
    begin((q_ref, rlow_ref, rhigh_ref, d_ref, near_ref, wt_ref, wl_ref), v, v + force_ref[0], outs[:4], outs[4])


def again_kernel(scal_ref, q_ref, rlow_ref, rhigh_ref, d_ref, near_ref, wt_ref, wl_ref, anchor_ref, force_ref, *refs):
    ends, outs = refs[:-5], refs[-5:]
    turn = scal_ref[2]
    before = jnp.zeros((DOFS, ELEMS), F32)
    for k, end_ref in enumerate(ends):
        before = jnp.where(turn == k, end_ref[...], before)
    v = anchor_ref[...] + before
    begin((q_ref, rlow_ref, rhigh_ref, d_ref, near_ref, wt_ref, wl_ref), v, v + force_ref[0], outs[:4], outs[4])


def fine_kernel(step, keep, scal_ref, q_ref, rlow_ref, rhigh_ref, d_ref, near_ref, wt_ref, wl_ref,
                below_ref, above_ref, bin_ref, uin_ref, kx_ref, force_ref, *outs):
    w = (q_ref, rlow_ref, rhigh_ref, d_ref, near_ref, wt_ref, wl_ref)
    v = finish(scal_ref, w, below_ref, above_ref, 0, uin_ref, bin_ref, kx_ref, outs[-1])
    begin(w, v, v + force_ref[step], outs[:4], outs[-1])
    if keep:
        outs[4][...] = v


def residual_kernel(scal_ref, q_ref, rlow_ref, rhigh_ref, d_ref, near_ref, wt_ref, wl_ref,
                    below_ref, above_ref, bin_ref, uin_ref, kx_ref, guess_ref, v_ref, rows_ref):
    w = (q_ref, rlow_ref, rhigh_ref, d_ref, near_ref, wt_ref, wl_ref)
    v = finish(scal_ref, w, below_ref, above_ref, 0, uin_ref, bin_ref, kx_ref, rows_ref)
    v_ref[...] = v - guess_ref[...]


def last_kernel(scal_ref, q_ref, rlow_ref, rhigh_ref, d_ref, near_ref, wt_ref, wl_ref,
                below_ref, above_ref, bin_ref, uin_ref, kx_ref, guess_ref, back0_ref, back1_ref, v1_ref, v2_ref, *refs):
    ends, (out_ref, rows_ref) = refs[:-2], refs[-2:]
    w = (q_ref, rlow_ref, rhigh_ref, d_ref, near_ref, wt_ref, wl_ref)
    v = finish(scal_ref, w, below_ref, above_ref, 0, uin_ref, bin_ref, kx_ref, rows_ref)
    out_ref[0] = reorder(v1_ref[...], back0_ref, back1_ref)
    out_ref[1] = reorder(v2_ref[...], back0_ref, back1_ref)
    out_ref[2] = reorder(v, back0_ref, back1_ref)
    turn = scal_ref[3]
    after = jnp.zeros((DOFS, ELEMS), F32)
    for k, end_ref in enumerate(ends):
        after = jnp.where(turn == k, end_ref[...], after)
    out_ref[3] = reorder(guess_ref[...] + after, back0_ref, back1_ref)


def start_kernel(q_ref, rlow_ref, rhigh_ref, d_ref, near_ref, wt_ref, wl_ref, v_ref, *outs):
    v = v_ref[...]
    begin((q_ref, rlow_ref, rhigh_ref, d_ref, near_ref, wt_ref, wl_ref), v, v, outs[:4], outs[4])


def turn_kernel(turn, first, more, scal_ref, q_ref, rlow_ref, rhigh_ref, d_ref, near_ref, wt_ref, wl_ref,
                below_ref, above_ref, bin_ref, uin_ref, kx_ref, res_ref, *outs):
    w = (q_ref, rlow_ref, rhigh_ref, d_ref, near_ref, wt_ref, wl_ref)
    v = finish(scal_ref, w, below_ref, above_ref, first, uin_ref, bin_ref, kx_ref, outs[-1])
    v = v + res_ref[scal_ref[5 + turn]]
    if more:
        begin(w, v, v, outs[:4], outs[4])
    else:
        outs[0][...] = v


STATE = ((DOFS, ELEMS), F32)
EDGE = ((2 * TRACE, LANES), F32)
FACES = ((TRACE // 2 * TRACE, LANES), F32)
EDGES = ((TRACE * DOFS, LANES), F32)
INVERSE = ((DOFS, DOFS, ELEMS), F32)
ROWS = pltpu.VMEM((DOFS, ELEMS), F32)
FACE_ROWS = pltpu.VMEM((TRACE, ELEMS), F32)
BEGUN = (STATE, STATE, EDGE, EDGE)
VMEM_LIMIT = 4 << 20


def near_by(x):
    return pltpu.with_memory_space_constraint(x, pltpu.VMEM)


def far_off(x):
    return pltpu.with_memory_space_constraint(x, pltpu.HBM)


def call(kernel, outs, scratch, *args, scalars=True, hbm_in=(), hbm_out=(), windows=(), limit=VMEM_LIMIT, busy=None):
    specs = [VMEM] * len(args)
    if scalars:
        specs[0] = SMEM
    for n in hbm_in:
        specs[n] = ANY
    return pl.pallas_call(
        kernel,
        out_shape=[(pltpu.HBM if n in (*hbm_out, *windows) else pltpu.VMEM)(*x) for n, x in enumerate(outs)],
        in_specs=specs,
        out_specs=[ANY if n in hbm_out else VMEM for n in range(len(outs))],
        scratch_shapes=scratch,
        compiler_params=pltpu.CompilerParams(vmem_limit_bytes=limit),
        cost_estimate=None if busy is None else pl.CostEstimate(flops=0, bytes_accessed=busy, transcendentals=0),
    )(*args)


class Operator:
    def __init__(self, inverse, rest, stream):
        self.inverse, self.rest, self.stream = inverse, rest, stream

    def call(self, kernel, outs, *args, scal=None, final=False, far=()):
        lead = [] if scal is None else [scal]
        fixed = [self.inverse, *self.rest]
        place, stream = len(lead), self.stream
        args = lead + fixed + list(args)
        specs = [SMEM] * place + [VMEM] * (len(args) - place)
        for n in range(place, len(args)):
            if n == place and stream:
                args[n] = far_off(args[n])
                specs[n] = ANY
            elif n - place - len(fixed) not in far:
                args[n] = near_by(args[n])

        def body(*refs):
            refs = list(refs)
            if stream:
                refs, (target, sems) = refs[:-2], refs[-2:]
                refs[place] = Stream(refs[place], target, sems)
            kernel(*refs)

        kind = jax.ShapeDtypeStruct if final else pltpu.VMEM
        fetch = [pltpu.VMEM((DOFS, DOFS, ELEMS), F32), pltpu.SemaphoreType.DMA((PARTS,))] if stream else []
        return pl.pallas_call(
            body,
            out_shape=[kind(*x) for x in outs],
            in_specs=specs,
            out_specs=[VMEM] * len(outs),
            scratch_shapes=[ROWS] + fetch,
            compiler_params=pltpu.CompilerParams(vmem_limit_bytes=(8 << 20) if stream else VMEM_LIMIT),
        )(*args)


def local(
    initial,
    guess,
    forcing,
    fine_inverse,
    coarse_inverse,
    neighbour,
    send_low,
    send_high,
    trace_map,
    lift_map,
):
    times = lax.axis_size("tm")
    blocks = lax.axis_size("space")
    now = lax.axis_index("tm")
    place = lax.axis_index("space")
    guess = guess[0]

    def route(target):
        return [
            (t * blocks + s, a * blocks + b)
            for t in range(times)
            for s in range(blocks)
            for a, b in [target(t, s)]
        ]

    def shift(by, flip=0):
        def target(t, s):
            there = s + by
            t = t ^ flip
            return (t if 0 <= there < blocks else t ^ HALF), there % blocks

        return route(target)

    up, down = shift(1), shift(-1)
    chain_up, chain_down = shift(1, 1), shift(-1, 1)
    swap_cores = route(lambda t, s: (t ^ 1, s))
    swap_halves = route(lambda t, s: (t ^ HALF, s))

    def move(x, pairs):
        return lax.ppermute(x, ("tm", "space"), pairs)

    def exchange(low, high, up=up, down=down):
        above = move(low, down)
        below = move(high, up)
        return below, above

    group, core = now % HALF // 2, now % 2
    turns = jnp.arange(HALF)
    slots = (group - turns // 2) % 4 + 4 * (turns % 2 ^ core)
    early = now < HALF
    turn = now % HALF
    before = jnp.where(early, turn - 1, HALF + turn)
    after = jnp.where(early, turn, HALF + turn + 1)
    scal = jnp.concatenate([jnp.stack([place > 0, place < blocks - 1, before, after, core]), slots]).astype(jnp.int32)

    slow, shigh = send_low.reshape(1, LANES), send_high.reshape(1, LANES)
    traces = trace_map.reshape(6 * TRACE, DOFS)
    lifts = jnp.transpose(lift_map, (0, 2, 1)).reshape(6 * TRACE, DOFS)
    ahead = [(i, i + 1) for i in range(times - 1)]
    moved = lax.ppermute(guess, "tm", ahead)

    def prepare(inverse, scal, windows=()):
        q, d, rlow, rhigh, klow, khigh = call(
            prepare_kernel,
            [INVERSE, STATE, EDGES, EDGES, FACES, FACES],
            [pltpu.VMEM((DOFS, DOFS, ELEMS), F32)] + [pltpu.SemaphoreType.DMA((DOFS // 8,))] * 2,
            scal, *map(far_off, (inverse, slow, shigh, traces, lifts)),
            hbm_in=(1,), hbm_out=(0,), windows=windows, limit=10 << 20, busy=24 << 20,
        )
        return q, (rlow, rhigh, d), (klow, khigh)

    def both_halves(faces):
        return (*faces, *[move(x, swap_cores) for x in faces])

    def cross(faces, low, high):
        args = [near_by(x) for x in (*faces, low, high)]
        (kx,) = call(cross_kernel, [EDGE], [FACE_ROWS], scal, *args, busy=2 << 20)
        return kx

    fine_inverse, fine_rest, fine_faces = prepare(fine_inverse, scal)
    fine_faces = exchange(*fine_faces)
    wt, wl, near, back0, back1 = call(
        tables_kernel,
        [((192, 192), BF16), ((64, 576), BF16), ((16, LANES), jnp.int32), ((1, LANES), jnp.int32), ((1, LANES), jnp.int32)],
        [],
        *map(far_off, (traces, jnp.transpose(lift_map, (1, 0, 2)).reshape(DOFS, 6 * TRACE), neighbour, slow, shigh)),
        scalars=False,
    )
    forces, goal = call(
        reorder_kernel, [((4, DOFS, ELEMS), F32), STATE], [], *map(far_off, (forcing, guess, slow, shigh)), scalars=False
    )
    fine = Operator(fine_inverse, (*fine_rest, near, wt, wl), False)
    start = jnp.where(now == 0, initial, moved)
    anchor, b, u, low, high = fine.call(
        first_kernel, [STATE, *BEGUN], start, far_off(slow), far_off(shigh), forces, far=(0, 1, 2)
    )
    low, later = lax.optimization_barrier((low, scal))
    coarse_inverse, coarse_rest, coarse_faces = prepare(coarse_inverse, later, (2, 3, 4, 5))
    fine_faces = both_halves(lax.optimization_barrier((*fine_faces, coarse_rest[2]))[:2])

    def fine_step(step, keep, b, u, low, high):
        kx = cross(fine_faces, low, high)
        below, above = exchange(low, high)
        return fine.call(
            functools.partial(fine_kernel, step, keep), [*BEGUN, STATE] if keep else BEGUN,
            below, above, b, u, kx, forces, scal=scal,
        )

    for step in (1, 2, 3):
        b, u, low, high = fine_step(step, False, b, u, low, high)
    kx = cross(fine_faces, low, high)
    below, above = exchange(low, high)
    (residual,) = fine.call(residual_kernel, [STATE], below, above, b, u, kx, goal, scal=scal)

    residual, coarse_inverse, coarse_rest, coarse_faces = lax.optimization_barrier(
        (residual, coarse_inverse, coarse_rest, coarse_faces)
    )
    coarse = Operator(coarse_inverse, (*coarse_rest, near, wt, wl), False)
    coarse_faces = both_halves(exchange(*coarse_faces))

    def turned(k):
        return route(lambda t, s: (t // HALF * HALF + (t % HALF + 2 * k) % HALF, s))

    held = jnp.stack([residual] + [move(residual, turned(k)) for k in (1, 2, 3)])
    held = jnp.concatenate([held, move(held, swap_cores)])

    def chain(first, count, b, u, low, high, edges=None):
        ends = []
        for turn in range(first, first + count):
            kx = cross(coarse_faces, low, high)
            below, above = exchange(low, high, chain_up, chain_down) if edges is None else edges
            edges = None
            b, u, low, high = coarse.call(
                functools.partial(turn_kernel, turn, 0, True), BEGUN, below, above, b, u, kx, held, scal=scal
            )
            ends.append(b)
        return ends, (b, u, low, high)

    base = lax.dynamic_index_in_dim(held, scal[5], 0, False)
    early_ends, (b, u, low, high) = chain(1, HALF - 1, *coarse.call(start_kernel, BEGUN, base))
    early_ends = [base] + early_ends
    edges = exchange(low, high, shift(1, HALF + 1), shift(-1, HALF + 1))
    late_start = move(b, swap_halves)
    late_ends, (cb, cu, clow, chigh) = chain(0, HALF - 1, *coarse.call(start_kernel, BEGUN, late_start), edges)
    late_ends = [late_start] + late_ends

    b, u, low, high = fine.call(again_kernel, BEGUN, anchor, forces, *early_ends, *late_ends, scal=scal)
    ckx = cross(coarse_faces, clow, chigh)
    kx = cross(fine_faces, low, high)
    below, above = exchange(jnp.concatenate([low, clow]), jnp.concatenate([high, chigh]))
    b, u, low, high, v1 = fine.call(
        functools.partial(fine_kernel, 1, True), [*BEGUN, STATE], below, above, b, u, kx, forces, scal=scal
    )
    (last_end,) = coarse.call(
        functools.partial(turn_kernel, HALF - 1, 2 * TRACE, False), [STATE], below, above, cb, cu, ckx, held, scal=scal
    )
    b, u, low, high, v2 = fine_step(2, True, b, u, low, high)
    kx = cross(fine_faces, low, high)
    below, above = exchange(low, high)
    (out,) = fine.call(
        last_kernel, [((4, DOFS, ELEMS), F32)],
        below, above, b, u, kx, goal, back0, back1, v1, v2, *early_ends, *late_ends, last_end,
        scal=scal, final=True,
    )
    return out


def solution(mesh):
    in_specs = (
        P(None, "space"),
        P("tm", None, "space"),
        P("tm", None, "space"),
        P(None, None, "space"),
        P(None, None, "space"),
        P(None, "space"),
        P("space"),
        P("space"),
        P(),
        P(),
    )
    out_specs = P("tm", None, "space")
    return jax.shard_map(local, mesh=mesh, in_specs=in_specs, out_specs=out_specs, check_vma=False)
```

```python
import functools

import jax
import jax.numpy as jnp
from jax import lax
from jax.experimental import pallas as pl
from jax.experimental.pallas import tpu as pltpu
from jax.sharding import PartitionSpec as P

DOFS = 64
TRACE = 32
LANES = 128
ELEMS = 256
HALF = 8
PARTS = 4
F32 = jnp.float32
BF16 = jnp.bfloat16

VMEM = pl.BlockSpec(memory_space=pltpu.VMEM)
SMEM = pl.BlockSpec(memory_space=pltpu.SMEM)
ANY = pl.BlockSpec(memory_space=pl.ANY)


class Stream:
    def __init__(self, source, target, sems):
        self.target, self.copies = target, []
        for c in range(PARTS):
            rows = pl.ds(c * (DOFS // PARTS), DOFS // PARTS)
            self.copies.append(pltpu.make_async_copy(source.at[rows], target.at[rows], sems.at[c]))
            self.copies[-1].start()

    def ready(self):
        for copy in self.copies:
            copy.wait()
        self.copies = []
        return self.target


def halves(x):
    high = x.astype(BF16)
    return high, (x - high.astype(F32)).astype(BF16)


def dot(a, b):
    return jnp.dot(a, b, preferred_element_type=F32)


def dot3(weights, x):
    high, low = halves(x)
    return dot(weights, jnp.concatenate([high, low, high], axis=0))


def split_weights(w):
    high, low = halves(w)
    return jnp.concatenate([high.astype(F32), high.astype(F32), low.astype(F32)], axis=1).astype(BF16)


def pick(source, lane):
    lane = jnp.broadcast_to(lane, source.shape)
    return jnp.take_along_axis(source, lane, axis=1, mode="promise_in_bounds")


def pick_wide(source, index):
    lane = index & (LANES - 1)
    first, second = pick(source[:, :LANES], lane), pick(source[:, LANES:], lane)
    return jnp.where(jnp.broadcast_to(index, first.shape) < LANES, first, second)


def reorder(source, first_ref, second_ref):
    return jnp.concatenate([pick_wide(source, first_ref[...]), pick_wide(source, second_ref[...])], axis=1)


def gathered(traces, below, above, near_ref):
    nothing = jnp.zeros((TRACE, LANES), F32)
    rows = []
    for face in range(6):
        first = (face ^ 1) * TRACE
        low = traces[first : first + TRACE, :LANES]
        high = traces[first : first + TRACE, LANES:]
        if face == 0:
            pair = [nothing if below is None else below, pick(low, near_ref[0:1, :])]
        elif face == 1:
            pair = [pick(high, near_ref[1:2, :]), nothing if above is None else above]
        else:
            pair = [pick(low, near_ref[2 * face - 2 : 2 * face - 1, :]), pick(high, near_ref[2 * face - 1 : 2 * face, :])]
        rows.append(jnp.concatenate(pair, axis=1))
    return jnp.concatenate(rows, axis=0)


def apply_inverse(q_ref, d_ref, rows_ref, right):
    rows_ref[...] = right
    if isinstance(q_ref, Stream):
        q_ref = q_ref.ready()

    def step(chunk, total):
        for k in range(8):
            j = chunk * 8 + k
            total = total - q_ref[j] * rows_ref[pl.ds(j, 1), :]
        return total

    return lax.fori_loop(0, DOFS // 8, step, 2.0 * d_ref[...] * right)


def apply_edges(low_ref, high_ref, rows_ref, below, above, start):
    rows_ref[:TRACE, :LANES] = below
    rows_ref[:TRACE, LANES:] = above

    def step(chunk, total):
        low, high = total
        tile = rows_ref[pl.ds(pl.multiple_of(chunk * 8, 8), 8), :]
        for k in range(8):
            u = chunk * 8 + k
            block = pl.ds(pl.multiple_of(u * DOFS, DOFS), DOFS)
            low = low - low_ref[block, :] * tile[k : k + 1, :LANES]
            high = high - high_ref[block, :] * tile[k : k + 1, LANES:]
        return low, high

    total = lax.fori_loop(0, TRACE // 8, step, (start[:, :LANES], start[:, LANES:]))
    return jnp.concatenate(total, axis=1)


def tables_kernel(trace_ref, lift_ref, nbr_ref, slow_ref, shigh_ref, wt_ref, wl_ref, near_ref, back0_ref, back1_ref):
    wt_ref[...] = split_weights(trace_ref[...])
    wl_ref[...] = split_weights(lift_ref[...])
    sends = (slow_ref, shigh_ref)
    position = lax.broadcasted_iota(jnp.int32, (LANES, LANES), 0)
    lane = lax.broadcasted_iota(jnp.int32, (LANES, LANES), 1)
    places = []
    for half in range(2):
        place = jnp.zeros((1, LANES), F32)
        for layer in range(2):
            ids = jnp.broadcast_to(sends[layer][...], (LANES, LANES)).astype(F32)
            ids = jnp.transpose(ids).astype(jnp.int32)
            here = jnp.where(ids == lane + half * LANES, position + layer * LANES, 0).astype(F32)
            place = place + jnp.sum(here, axis=0, keepdims=True)
        places.append(place.astype(jnp.int32))
    back0_ref[...] = places[0]
    back1_ref[...] = places[1]
    place = jnp.broadcast_to(jnp.concatenate(places, axis=1), (8, ELEMS))
    order = [(0, 1), (1, 0)] + [(face, layer) for face in range(2, 6) for layer in range(2)]
    for row, (face, layer) in enumerate(order):
        ids = pick_wide(jnp.broadcast_to(nbr_ref[face : face + 1, :], (8, ELEMS)), sends[layer][...])
        near_ref[row : row + 1, :] = (pick_wide(place, ids[0:1]) & (LANES - 1))[0:1]


def prepare_kernel(scal_ref, q_ref, slow_ref, shigh_ref, trace_ref, lift_ref,
                   out_ref, d_ref, rlow_ref, rhigh_ref, klow_ref, khigh_ref, held_ref, sems, out_sems):
    def fetch(c):
        rows = pl.ds(c * 8, 8)
        return pltpu.make_async_copy(q_ref.at[rows], held_ref.at[rows], sems.at[c])

    def put(c):
        rows = pl.ds(c * 8, 8)
        return pltpu.make_async_copy(held_ref.at[rows], out_ref.at[rows], out_sems.at[c])

    for c in range(DOFS // 8):
        fetch(c).start()
    lift = split_weights(lift_ref[: 2 * TRACE, :])
    tr = split_weights(trace_ref[: 2 * TRACE, :])

    def chunk(c, carry):
        fetch(c).wait()
        for k in range(8):
            i = c * 8 + k
            q = reorder(held_ref[i], slow_ref, shigh_ref)
            held_ref[i] = q
            d_ref[pl.ds(i, 1), :] = held_ref[i, pl.ds(i, 1), :]
            r = dot3(lift, q)
            place = pl.ds(i, TRACE, stride=DOFS)
            rlow_ref[place, :] = r[:TRACE, :LANES]
            rhigh_ref[place, :] = r[TRACE:, LANES:]
        put(c).start()
        return carry

    lax.fori_loop(0, DOFS // 8, chunk, 0)
    first = scal_ref[4] * (TRACE // 2)

    def faces(c, carry):
        for k in range(4):
            n = c * 4 + k
            rows = pl.ds(pl.multiple_of((first + n) * DOFS, DOFS), DOFS)
            made = dot3(tr, jnp.concatenate([rlow_ref[rows, :], rhigh_ref[rows, :]], axis=1))
            place = pl.ds(pl.multiple_of(n * TRACE, TRACE), TRACE)
            klow_ref[place, :] = made[:TRACE, :LANES]
            khigh_ref[place, :] = made[TRACE:, LANES:]
        return carry

    lax.fori_loop(0, TRACE // 8, faces, 0)
    for c in range(DOFS // 8):
        put(c).wait()


def reorder_kernel(force_ref, guess_ref, slow_ref, shigh_ref, force_out_ref, guess_out_ref):
    for step in range(4):
        force_out_ref[step] = reorder(force_ref[step], slow_ref, shigh_ref)
    guess_out_ref[...] = reorder(guess_ref[...], slow_ref, shigh_ref)


def finish(scal_ref, w, below_ref, above_ref, first, u_ref, b_ref, kx_ref, rows_ref):
    q_ref, rlow_ref, rhigh_ref, d_ref, near_ref, wt_ref, wl_ref = w
    below = jnp.where(scal_ref[0] == 1, below_ref[first : first + 2 * TRACE, :], 0.0)
    above = jnp.where(scal_ref[1] == 1, above_ref[first : first + 2 * TRACE, :], 0.0)
    v1 = apply_edges(rlow_ref, rhigh_ref, rows_ref, below[TRACE:], above[TRACE:], u_ref[...])
    traces = dot3(wt_ref[...], v1)
    below = below[:TRACE] - kx_ref[:TRACE, :]
    above = above[:TRACE] - kx_ref[TRACE:, :]
    coupled = dot3(wl_ref[...], gathered(traces, below, above, near_ref))
    return apply_inverse(q_ref, d_ref, rows_ref, b_ref[...] - coupled)


def begin(w, v, b, outs, rows_ref):
    q_ref, rlow_ref, rhigh_ref, d_ref, near_ref, wt_ref, wl_ref = w
    b_ref, u_ref, low_ref, high_ref = outs
    traces = dot3(wt_ref[...], v)
    coupled = dot3(wl_ref[...], gathered(traces, None, None, near_ref))
    u = apply_inverse(q_ref, d_ref, rows_ref, b - coupled)
    ends = dot3(wt_ref[: 2 * TRACE, :], u)
    b_ref[...] = b
    u_ref[...] = u
    low_ref[:TRACE, :] = ends[:TRACE, :LANES]
    low_ref[TRACE:, :] = traces[:TRACE, :LANES]
    high_ref[:TRACE, :] = ends[TRACE:, LANES:]
    high_ref[TRACE:, :] = traces[TRACE : 2 * TRACE, LANES:]


def cross_kernel(scal_ref, kb0_ref, ka0_ref, kb1_ref, ka1_ref, low_ref, high_ref, kx_ref, rows_ref):
    rows_ref[:, :LANES] = low_ref[TRACE:, :]
    rows_ref[:, LANES:] = high_ref[TRACE:, :]
    half = TRACE // 2

    def step(chunk, total):
        below, above = total
        for kb_ref, ka_ref, core in ((kb0_ref, ka0_ref, scal_ref[4]), (kb1_ref, ka1_ref, 1 - scal_ref[4])):
            tile = rows_ref[pl.ds(pl.multiple_of(core * half + chunk * 8, 8), 8), :]
            for k in range(8):
                place = pl.ds(pl.multiple_of((chunk * 8 + k) * TRACE, TRACE), TRACE)
                below = below + kb_ref[place, :] * tile[k : k + 1, :LANES]
                above = above + ka_ref[place, :] * tile[k : k + 1, LANES:]
        return below, above

    nothing = jnp.zeros((TRACE, LANES), F32)
    below, above = lax.fori_loop(0, half // 8, step, (nothing, nothing))
    kx_ref[:TRACE, :] = jnp.where(scal_ref[0] == 1, below, 0.0)
    kx_ref[TRACE:, :] = jnp.where(scal_ref[1] == 1, above, 0.0)


def first_kernel(q_ref, rlow_ref, rhigh_ref, d_ref, near_ref, wt_ref, wl_ref, anchor_ref, slow_ref, shigh_ref, force_ref, v_ref, *outs):
    v = reorder(anchor_ref[...], slow_ref, shigh_ref)
    v_ref[...] = v
    begin((q_ref, rlow_ref, rhigh_ref, d_ref, near_ref, wt_ref, wl_ref), v, v + force_ref[0], outs[:4], outs[4])


def again_kernel(scal_ref, q_ref, rlow_ref, rhigh_ref, d_ref, near_ref, wt_ref, wl_ref, anchor_ref, force_ref, *refs):
    ends, outs = refs[:-5], refs[-5:]
    turn = scal_ref[2]
    before = jnp.zeros((DOFS, ELEMS), F32)
    for k, end_ref in enumerate(ends):
        before = jnp.where(turn == k, end_ref[...], before)
    v = anchor_ref[...] + before
    begin((q_ref, rlow_ref, rhigh_ref, d_ref, near_ref, wt_ref, wl_ref), v, v + force_ref[0], outs[:4], outs[4])


def fine_kernel(step, keep, scal_ref, q_ref, rlow_ref, rhigh_ref, d_ref, near_ref, wt_ref, wl_ref,
                below_ref, above_ref, bin_ref, uin_ref, kx_ref, force_ref, *outs):
    w = (q_ref, rlow_ref, rhigh_ref, d_ref, near_ref, wt_ref, wl_ref)
    v = finish(scal_ref, w, below_ref, above_ref, 0, uin_ref, bin_ref, kx_ref, outs[-1])
    begin(w, v, v + force_ref[step], outs[:4], outs[-1])
    if keep:
        outs[4][...] = v


def residual_kernel(scal_ref, q_ref, rlow_ref, rhigh_ref, d_ref, near_ref, wt_ref, wl_ref,
                    below_ref, above_ref, bin_ref, uin_ref, kx_ref, guess_ref, v_ref, rows_ref):
    w = (q_ref, rlow_ref, rhigh_ref, d_ref, near_ref, wt_ref, wl_ref)
    v = finish(scal_ref, w, below_ref, above_ref, 0, uin_ref, bin_ref, kx_ref, rows_ref)
    v_ref[...] = v - guess_ref[...]


def last_kernel(scal_ref, q_ref, rlow_ref, rhigh_ref, d_ref, near_ref, wt_ref, wl_ref,
                below_ref, above_ref, bin_ref, uin_ref, kx_ref, guess_ref, back0_ref, back1_ref, v1_ref, v2_ref, *refs):
    ends, (out_ref, rows_ref) = refs[:-2], refs[-2:]
    w = (q_ref, rlow_ref, rhigh_ref, d_ref, near_ref, wt_ref, wl_ref)
    v = finish(scal_ref, w, below_ref, above_ref, 0, uin_ref, bin_ref, kx_ref, rows_ref)
    out_ref[0] = reorder(v1_ref[...], back0_ref, back1_ref)
    out_ref[1] = reorder(v2_ref[...], back0_ref, back1_ref)
    out_ref[2] = reorder(v, back0_ref, back1_ref)
    turn = scal_ref[3]
    after = jnp.zeros((DOFS, ELEMS), F32)
    for k, end_ref in enumerate(ends):
        after = jnp.where(turn == k, end_ref[...], after)
    out_ref[3] = reorder(guess_ref[...] + after, back0_ref, back1_ref)


def start_kernel(q_ref, rlow_ref, rhigh_ref, d_ref, near_ref, wt_ref, wl_ref, v_ref, *outs):
    v = v_ref[...]
    begin((q_ref, rlow_ref, rhigh_ref, d_ref, near_ref, wt_ref, wl_ref), v, v, outs[:4], outs[4])


def turn_kernel(turn, first, more, scal_ref, q_ref, rlow_ref, rhigh_ref, d_ref, near_ref, wt_ref, wl_ref,
                below_ref, above_ref, bin_ref, uin_ref, kx_ref, res_ref, *outs):
    w = (q_ref, rlow_ref, rhigh_ref, d_ref, near_ref, wt_ref, wl_ref)
    v = finish(scal_ref, w, below_ref, above_ref, first, uin_ref, bin_ref, kx_ref, outs[-1])
    v = v + res_ref[scal_ref[5 + turn]]
    if more:
        begin(w, v, v, outs[:4], outs[4])
    else:
        outs[0][...] = v


STATE = ((DOFS, ELEMS), F32)
EDGE = ((2 * TRACE, LANES), F32)
FACES = ((TRACE // 2 * TRACE, LANES), F32)
EDGES = ((TRACE * DOFS, LANES), F32)
INVERSE = ((DOFS, DOFS, ELEMS), F32)
ROWS = pltpu.VMEM((DOFS, ELEMS), F32)
FACE_ROWS = pltpu.VMEM((TRACE, ELEMS), F32)
BEGUN = (STATE, STATE, EDGE, EDGE)
VMEM_LIMIT = 4 << 20


def near_by(x):
    return pltpu.with_memory_space_constraint(x, pltpu.VMEM)


def far_off(x):
    return pltpu.with_memory_space_constraint(x, pltpu.HBM)


def call(kernel, outs, scratch, *args, scalars=True, hbm_in=(), hbm_out=(), windows=(), limit=VMEM_LIMIT, busy=None):
    specs = [VMEM] * len(args)
    if scalars:
        specs[0] = SMEM
    for n in hbm_in:
        specs[n] = ANY
    return pl.pallas_call(
        kernel,
        out_shape=[(pltpu.HBM if n in (*hbm_out, *windows) else pltpu.VMEM)(*x) for n, x in enumerate(outs)],
        in_specs=specs,
        out_specs=[ANY if n in hbm_out else VMEM for n in range(len(outs))],
        scratch_shapes=scratch,
        compiler_params=pltpu.CompilerParams(vmem_limit_bytes=limit),
        cost_estimate=None if busy is None else pl.CostEstimate(flops=0, bytes_accessed=busy, transcendentals=0),
    )(*args)


class Operator:
    def __init__(self, inverse, rest, stream):
        self.inverse, self.rest, self.stream = inverse, rest, stream

    def call(self, kernel, outs, *args, scal=None, final=False, far=()):
        lead = [] if scal is None else [scal]
        fixed = [self.inverse, *self.rest]
        place, stream = len(lead), self.stream
        args = lead + fixed + list(args)
        specs = [SMEM] * place + [VMEM] * (len(args) - place)
        for n in range(place, len(args)):
            if n == place and stream:
                args[n] = far_off(args[n])
                specs[n] = ANY
            elif n - place - len(fixed) not in far:
                args[n] = near_by(args[n])

        def body(*refs):
            refs = list(refs)
            if stream:
                refs, (target, sems) = refs[:-2], refs[-2:]
                refs[place] = Stream(refs[place], target, sems)
            kernel(*refs)

        kind = jax.ShapeDtypeStruct if final else pltpu.VMEM
        fetch = [pltpu.VMEM((DOFS, DOFS, ELEMS), F32), pltpu.SemaphoreType.DMA((PARTS,))] if stream else []
        return pl.pallas_call(
            body,
            out_shape=[kind(*x) for x in outs],
            in_specs=specs,
            out_specs=[VMEM] * len(outs),
            scratch_shapes=[ROWS] + fetch,
            compiler_params=pltpu.CompilerParams(vmem_limit_bytes=(8 << 20) if stream else VMEM_LIMIT),
        )(*args)


def local(
    initial,
    guess,
    forcing,
    fine_inverse,
    coarse_inverse,
    neighbour,
    send_low,
    send_high,
    trace_map,
    lift_map,
):
    times = lax.axis_size("tm")
    blocks = lax.axis_size("space")
    now = lax.axis_index("tm")
    place = lax.axis_index("space")
    guess = guess[0]

    def route(target):
        return [
            (t * blocks + s, a * blocks + b)
            for t in range(times)
            for s in range(blocks)
            for a, b in [target(t, s)]
        ]

    def shift(by, flip=0):
        def target(t, s):
            there = s + by
            t = t ^ flip
            return (t if 0 <= there < blocks else t ^ HALF), there % blocks

        return route(target)

    up, down = shift(1), shift(-1)
    chain_up, chain_down = shift(1, 1), shift(-1, 1)
    swap_cores = route(lambda t, s: (t ^ 1, s))
    swap_halves = route(lambda t, s: (t ^ HALF, s))

    def move(x, pairs):
        return lax.ppermute(x, ("tm", "space"), pairs)

    def exchange(low, high, up=up, down=down):
        above = move(low, down)
        below = move(high, up)
        return below, above

    group, core = now % HALF // 2, now % 2
    turns = jnp.arange(HALF)
    slots = (group - turns // 2) % 4 + 4 * (turns % 2 ^ core)
    early = now < HALF
    turn = now % HALF
    before = jnp.where(early, turn - 1, HALF + turn)
    after = jnp.where(early, turn, HALF + turn + 1)
    scal = jnp.concatenate([jnp.stack([place > 0, place < blocks - 1, before, after, core]), slots]).astype(jnp.int32)

    slow, shigh = send_low.reshape(1, LANES), send_high.reshape(1, LANES)
    traces = trace_map.reshape(6 * TRACE, DOFS)
    lifts = jnp.transpose(lift_map, (0, 2, 1)).reshape(6 * TRACE, DOFS)
    ahead = [(i, i + 1) for i in range(times - 1)]
    moved = lax.ppermute(guess, "tm", ahead)

    def prepare(inverse, scal, windows=()):
        q, d, rlow, rhigh, klow, khigh = call(
            prepare_kernel,
            [INVERSE, STATE, EDGES, EDGES, FACES, FACES],
            [pltpu.VMEM((DOFS, DOFS, ELEMS), F32)] + [pltpu.SemaphoreType.DMA((DOFS // 8,))] * 2,
            scal, *map(far_off, (inverse, slow, shigh, traces, lifts)),
            hbm_in=(1,), hbm_out=(0,), windows=windows, limit=10 << 20, busy=24 << 20,
        )
        return q, (rlow, rhigh, d), (klow, khigh)

    def both_halves(faces):
        return (*faces, *[move(x, swap_cores) for x in faces])

    def cross(faces, low, high):
        args = [near_by(x) for x in (*faces, low, high)]
        (kx,) = call(cross_kernel, [EDGE], [FACE_ROWS], scal, *args, busy=2 << 20)
        return kx

    fine_inverse, fine_rest, fine_faces = prepare(fine_inverse, scal)
    fine_faces = exchange(*fine_faces)
    wt, wl, near, back0, back1 = call(
        tables_kernel,
        [((192, 192), BF16), ((64, 576), BF16), ((16, LANES), jnp.int32), ((1, LANES), jnp.int32), ((1, LANES), jnp.int32)],
        [],
        *map(far_off, (traces, jnp.transpose(lift_map, (1, 0, 2)).reshape(DOFS, 6 * TRACE), neighbour, slow, shigh)),
        scalars=False,
    )
    forces, goal = call(
        reorder_kernel, [((4, DOFS, ELEMS), F32), STATE], [], *map(far_off, (forcing, guess, slow, shigh)), scalars=False
    )
    fine = Operator(fine_inverse, (*fine_rest, near, wt, wl), False)
    start = jnp.where(now == 0, initial, moved)
    anchor, b, u, low, high = fine.call(
        first_kernel, [STATE, *BEGUN], start, far_off(slow), far_off(shigh), forces, far=(0, 1, 2)
    )
    low, high, later = lax.optimization_barrier((low, high, scal))
    coarse_inverse, coarse_rest, coarse_faces = prepare(coarse_inverse, later, (2, 3, 4, 5))
    fine_faces = both_halves(lax.optimization_barrier((*fine_faces, coarse_rest[2]))[:2])

    def fine_step(step, keep, b, u, low, high):
        kx = cross(fine_faces, low, high)
        below, above = exchange(low, high)
        return fine.call(
            functools.partial(fine_kernel, step, keep), [*BEGUN, STATE] if keep else BEGUN,
            below, above, b, u, kx, forces, scal=scal,
        )

    for step in (1, 2, 3):
        b, u, low, high = fine_step(step, False, b, u, low, high)
    kx = cross(fine_faces, low, high)
    below, above = exchange(low, high)
    (residual,) = fine.call(residual_kernel, [STATE], below, above, b, u, kx, goal, scal=scal)

    residual, coarse_inverse, coarse_rest, coarse_faces = lax.optimization_barrier(
        (residual, coarse_inverse, coarse_rest, coarse_faces)
    )
    coarse = Operator(coarse_inverse, (*coarse_rest, near, wt, wl), False)
    coarse_faces = both_halves(exchange(*coarse_faces))

    def turned(k):
        return route(lambda t, s: (t // HALF * HALF + (t % HALF + 2 * k) % HALF, s))

    held = jnp.stack([residual] + [move(residual, turned(k)) for k in (1, 2, 3)])
    held = jnp.concatenate([held, move(held, swap_cores)])

    def chain(first, count, b, u, low, high, edges=None):
        ends = []
        for turn in range(first, first + count):
            kx = cross(coarse_faces, low, high)
            below, above = exchange(low, high, chain_up, chain_down) if edges is None else edges
            edges = None
            b, u, low, high = coarse.call(
                functools.partial(turn_kernel, turn, 0, True), BEGUN, below, above, b, u, kx, held, scal=scal
            )
            ends.append(b)
        return ends, (b, u, low, high)

    base = lax.dynamic_index_in_dim(held, scal[5], 0, False)
    early_ends, (b, u, low, high) = chain(1, HALF - 1, *coarse.call(start_kernel, BEGUN, base))
    early_ends = [base] + early_ends
    edges = exchange(low, high, shift(1, HALF + 1), shift(-1, HALF + 1))
    late_start = move(b, swap_halves)
    late_ends, (cb, cu, clow, chigh) = chain(0, HALF - 1, *coarse.call(start_kernel, BEGUN, late_start), edges)
    late_ends = [late_start] + late_ends

    b, u, low, high = fine.call(again_kernel, BEGUN, anchor, forces, *early_ends, *late_ends, scal=scal)
    ckx = cross(coarse_faces, clow, chigh)
    kx = cross(fine_faces, low, high)
    both = lax.optimization_barrier((jnp.concatenate([low, clow]), jnp.concatenate([high, chigh])))
    below, above = exchange(*both)
    b, u, low, high, v1 = fine.call(
        functools.partial(fine_kernel, 1, True), [*BEGUN, STATE], below, above, b, u, kx, forces, scal=scal
    )
    (last_end,) = coarse.call(
        functools.partial(turn_kernel, HALF - 1, 2 * TRACE, False), [STATE], below, above, cb, cu, ckx, held, scal=scal
    )
    b, u, low, high, v2 = fine_step(2, True, b, u, low, high)
    kx = cross(fine_faces, low, high)
    below, above = exchange(low, high)
    (out,) = fine.call(
        last_kernel, [((4, DOFS, ELEMS), F32)],
        below, above, b, u, kx, goal, back0, back1, v1, v2, *early_ends, *late_ends, last_end,
        scal=scal, final=True,
    )
    return out


def solution(mesh):
    in_specs = (
        P(None, "space"),
        P("tm", None, "space"),
        P("tm", None, "space"),
        P(None, None, "space"),
        P(None, None, "space"),
        P(None, "space"),
        P("space"),
        P("space"),
        P(),
        P(),
    )
    out_specs = P("tm", None, "space")
    return jax.shard_map(local, mesh=mesh, in_specs=in_specs, out_specs=out_specs, check_vma=False)
```

```python
import functools

import jax
import jax.numpy as jnp
from jax import lax
from jax.experimental import pallas as pl
from jax.experimental.pallas import tpu as pltpu
from jax.sharding import PartitionSpec as P

DOFS = 64
TRACE = 32
LANES = 128
ELEMS = 256
HALF = 8
PARTS = 4
F32 = jnp.float32
BF16 = jnp.bfloat16

VMEM = pl.BlockSpec(memory_space=pltpu.VMEM)
SMEM = pl.BlockSpec(memory_space=pltpu.SMEM)
ANY = pl.BlockSpec(memory_space=pl.ANY)


class Stream:
    def __init__(self, source, target, sems):
        self.target, self.copies = target, []
        for c in range(PARTS):
            rows = pl.ds(c * (DOFS // PARTS), DOFS // PARTS)
            self.copies.append(pltpu.make_async_copy(source.at[rows], target.at[rows], sems.at[c]))
            self.copies[-1].start()

    def ready(self):
        for copy in self.copies:
            copy.wait()
        self.copies = []
        return self.target


def halves(x):
    high = x.astype(BF16)
    return high, (x - high.astype(F32)).astype(BF16)


def dot(a, b):
    return jnp.dot(a, b, preferred_element_type=F32)


def dot3(weights, x):
    high, low = halves(x)
    return dot(weights, jnp.concatenate([high, low, high], axis=0))


def split_weights(w):
    high, low = halves(w)
    return jnp.concatenate([high.astype(F32), high.astype(F32), low.astype(F32)], axis=1).astype(BF16)


def pick(source, lane):
    lane = jnp.broadcast_to(lane, source.shape)
    return jnp.take_along_axis(source, lane, axis=1, mode="promise_in_bounds")


def pick_wide(source, index):
    lane = index & (LANES - 1)
    first, second = pick(source[:, :LANES], lane), pick(source[:, LANES:], lane)
    return jnp.where(jnp.broadcast_to(index, first.shape) < LANES, first, second)


def reorder(source, first_ref, second_ref):
    return jnp.concatenate([pick_wide(source, first_ref[...]), pick_wide(source, second_ref[...])], axis=1)


def gathered(traces, below, above, near_ref):
    nothing = jnp.zeros((TRACE, LANES), F32)
    rows = []
    for face in range(6):
        first = (face ^ 1) * TRACE
        low = traces[first : first + TRACE, :LANES]
        high = traces[first : first + TRACE, LANES:]
        if face == 0:
            pair = [nothing if below is None else below, pick(low, near_ref[0:1, :])]
        elif face == 1:
            pair = [pick(high, near_ref[1:2, :]), nothing if above is None else above]
        else:
            pair = [pick(low, near_ref[2 * face - 2 : 2 * face - 1, :]), pick(high, near_ref[2 * face - 1 : 2 * face, :])]
        rows.append(jnp.concatenate(pair, axis=1))
    return jnp.concatenate(rows, axis=0)


def apply_inverse(q_ref, d_ref, rows_ref, right):
    rows_ref[...] = right
    if isinstance(q_ref, Stream):
        q_ref = q_ref.ready()

    def step(chunk, total):
        for k in range(8):
            j = chunk * 8 + k
            total = total - q_ref[j] * rows_ref[pl.ds(j, 1), :]
        return total

    return lax.fori_loop(0, DOFS // 8, step, 2.0 * d_ref[...] * right)


def apply_edges(low_ref, high_ref, rows_ref, below, above, start):
    rows_ref[:TRACE, :LANES] = below
    rows_ref[:TRACE, LANES:] = above

    def step(chunk, total):
        low, high = total
        tile = rows_ref[pl.ds(pl.multiple_of(chunk * 8, 8), 8), :]
        for k in range(8):
            u = chunk * 8 + k
            block = pl.ds(pl.multiple_of(u * DOFS, DOFS), DOFS)
            low = low - low_ref[block, :] * tile[k : k + 1, :LANES]
            high = high - high_ref[block, :] * tile[k : k + 1, LANES:]
        return low, high

    total = lax.fori_loop(0, TRACE // 8, step, (start[:, :LANES], start[:, LANES:]))
    return jnp.concatenate(total, axis=1)


def tables_kernel(trace_ref, lift_ref, nbr_ref, slow_ref, shigh_ref, wt_ref, wl_ref, near_ref, back0_ref, back1_ref):
    wt_ref[...] = split_weights(trace_ref[...])
    wl_ref[...] = split_weights(lift_ref[...])
    sends = (slow_ref, shigh_ref)
    position = lax.broadcasted_iota(jnp.int32, (LANES, LANES), 0)
    lane = lax.broadcasted_iota(jnp.int32, (LANES, LANES), 1)
    places = []
    for half in range(2):
        place = jnp.zeros((1, LANES), F32)
        for layer in range(2):
            ids = jnp.broadcast_to(sends[layer][...], (LANES, LANES)).astype(F32)
            ids = jnp.transpose(ids).astype(jnp.int32)
            here = jnp.where(ids == lane + half * LANES, position + layer * LANES, 0).astype(F32)
            place = place + jnp.sum(here, axis=0, keepdims=True)
        places.append(place.astype(jnp.int32))
    back0_ref[...] = places[0]
    back1_ref[...] = places[1]
    place = jnp.broadcast_to(jnp.concatenate(places, axis=1), (8, ELEMS))
    order = [(0, 1), (1, 0)] + [(face, layer) for face in range(2, 6) for layer in range(2)]
    for row, (face, layer) in enumerate(order):
        ids = pick_wide(jnp.broadcast_to(nbr_ref[face : face + 1, :], (8, ELEMS)), sends[layer][...])
        near_ref[row : row + 1, :] = (pick_wide(place, ids[0:1]) & (LANES - 1))[0:1]


def prepare_kernel(scal_ref, q_ref, slow_ref, shigh_ref, trace_ref, lift_ref,
                   out_ref, d_ref, rlow_ref, rhigh_ref, klow_ref, khigh_ref, held_ref, sems, out_sems):
    def fetch(c):
        rows = pl.ds(c * 8, 8)
        return pltpu.make_async_copy(q_ref.at[rows], held_ref.at[rows], sems.at[c])

    def put(c):
        rows = pl.ds(c * 8, 8)
        return pltpu.make_async_copy(held_ref.at[rows], out_ref.at[rows], out_sems.at[c])

    for c in range(DOFS // 8):
        fetch(c).start()
    lift = split_weights(lift_ref[: 2 * TRACE, :])
    tr = split_weights(trace_ref[: 2 * TRACE, :])

    def chunk(c, carry):
        fetch(c).wait()
        for k in range(8):
            i = c * 8 + k
            q = reorder(held_ref[i], slow_ref, shigh_ref)
            held_ref[i] = q
            d_ref[pl.ds(i, 1), :] = held_ref[i, pl.ds(i, 1), :]
            r = dot3(lift, q)
            place = pl.ds(i, TRACE, stride=DOFS)
            rlow_ref[place, :] = r[:TRACE, :LANES]
            rhigh_ref[place, :] = r[TRACE:, LANES:]
        put(c).start()
        return carry

    lax.fori_loop(0, DOFS // 8, chunk, 0)
    first = scal_ref[4] * (TRACE // 2)

    def faces(c, carry):
        for k in range(4):
            n = c * 4 + k
            rows = pl.ds(pl.multiple_of((first + n) * DOFS, DOFS), DOFS)
            made = dot3(tr, jnp.concatenate([rlow_ref[rows, :], rhigh_ref[rows, :]], axis=1))
            place = pl.ds(pl.multiple_of(n * TRACE, TRACE), TRACE)
            klow_ref[place, :] = made[:TRACE, :LANES]
            khigh_ref[place, :] = made[TRACE:, LANES:]
        return carry

    lax.fori_loop(0, TRACE // 8, faces, 0)
    for c in range(DOFS // 8):
        put(c).wait()


def reorder_kernel(force_ref, guess_ref, slow_ref, shigh_ref, force_out_ref, guess_out_ref):
    for step in range(4):
        force_out_ref[step] = reorder(force_ref[step], slow_ref, shigh_ref)
    guess_out_ref[...] = reorder(guess_ref[...], slow_ref, shigh_ref)


def finish(scal_ref, w, below_ref, above_ref, first, u_ref, b_ref, kx_ref, rows_ref):
    q_ref, rlow_ref, rhigh_ref, d_ref, near_ref, wt_ref, wl_ref = w
    below = jnp.where(scal_ref[0] == 1, below_ref[first : first + 2 * TRACE, :], 0.0)
    above = jnp.where(scal_ref[1] == 1, above_ref[first : first + 2 * TRACE, :], 0.0)
    v1 = apply_edges(rlow_ref, rhigh_ref, rows_ref, below[TRACE:], above[TRACE:], u_ref[...])
    traces = dot3(wt_ref[...], v1)
    below = below[:TRACE] - kx_ref[:TRACE, :]
    above = above[:TRACE] - kx_ref[TRACE:, :]
    coupled = dot3(wl_ref[...], gathered(traces, below, above, near_ref))
    return apply_inverse(q_ref, d_ref, rows_ref, b_ref[...] - coupled)


def begin(w, v, b, outs, rows_ref):
    q_ref, rlow_ref, rhigh_ref, d_ref, near_ref, wt_ref, wl_ref = w
    b_ref, u_ref, low_ref, high_ref = outs
    traces = dot3(wt_ref[...], v)
    coupled = dot3(wl_ref[...], gathered(traces, None, None, near_ref))
    u = apply_inverse(q_ref, d_ref, rows_ref, b - coupled)
    ends = dot3(wt_ref[: 2 * TRACE, :], u)
    b_ref[...] = b
    u_ref[...] = u
    low_ref[:TRACE, :] = ends[:TRACE, :LANES]
    low_ref[TRACE:, :] = traces[:TRACE, :LANES]
    high_ref[:TRACE, :] = ends[TRACE:, LANES:]
    high_ref[TRACE:, :] = traces[TRACE : 2 * TRACE, LANES:]


def cross_kernel(scal_ref, kb0_ref, ka0_ref, kb1_ref, ka1_ref, low_ref, high_ref, kx_ref, rows_ref):
    rows_ref[:, :LANES] = low_ref[TRACE:, :]
    rows_ref[:, LANES:] = high_ref[TRACE:, :]
    half = TRACE // 2

    def step(chunk, total):
        below, above = total
        for kb_ref, ka_ref, core in ((kb0_ref, ka0_ref, scal_ref[4]), (kb1_ref, ka1_ref, 1 - scal_ref[4])):
            tile = rows_ref[pl.ds(pl.multiple_of(core * half + chunk * 8, 8), 8), :]
            for k in range(8):
                place = pl.ds(pl.multiple_of((chunk * 8 + k) * TRACE, TRACE), TRACE)
                below = below + kb_ref[place, :] * tile[k : k + 1, :LANES]
                above = above + ka_ref[place, :] * tile[k : k + 1, LANES:]
        return below, above

    nothing = jnp.zeros((TRACE, LANES), F32)
    below, above = lax.fori_loop(0, half // 8, step, (nothing, nothing))
    kx_ref[:TRACE, :] = jnp.where(scal_ref[0] == 1, below, 0.0)
    kx_ref[TRACE:, :] = jnp.where(scal_ref[1] == 1, above, 0.0)


def first_kernel(q_ref, rlow_ref, rhigh_ref, d_ref, near_ref, wt_ref, wl_ref, anchor_ref, slow_ref, shigh_ref, force_ref, v_ref, *outs):
    v = reorder(anchor_ref[...], slow_ref, shigh_ref)
    v_ref[...] = v
    begin((q_ref, rlow_ref, rhigh_ref, d_ref, near_ref, wt_ref, wl_ref), v, v + force_ref[0], outs[:4], outs[4])


def again_kernel(scal_ref, q_ref, rlow_ref, rhigh_ref, d_ref, near_ref, wt_ref, wl_ref, anchor_ref, force_ref, *refs):
    ends, outs = refs[:-5], refs[-5:]
    turn = scal_ref[2]
    before = jnp.zeros((DOFS, ELEMS), F32)
    for k, end_ref in enumerate(ends):
        before = jnp.where(turn == k, end_ref[...], before)
    v = anchor_ref[...] + before
    begin((q_ref, rlow_ref, rhigh_ref, d_ref, near_ref, wt_ref, wl_ref), v, v + force_ref[0], outs[:4], outs[4])


def fine_kernel(step, keep, scal_ref, q_ref, rlow_ref, rhigh_ref, d_ref, near_ref, wt_ref, wl_ref,
                below_ref, above_ref, bin_ref, uin_ref, kx_ref, force_ref, *outs):
    w = (q_ref, rlow_ref, rhigh_ref, d_ref, near_ref, wt_ref, wl_ref)
    v = finish(scal_ref, w, below_ref, above_ref, 0, uin_ref, bin_ref, kx_ref, outs[-1])
    begin(w, v, v + force_ref[step], outs[:4], outs[-1])
    if keep:
        outs[4][...] = v


def residual_kernel(scal_ref, q_ref, rlow_ref, rhigh_ref, d_ref, near_ref, wt_ref, wl_ref,
                    below_ref, above_ref, bin_ref, uin_ref, kx_ref, guess_ref, v_ref, rows_ref):
    w = (q_ref, rlow_ref, rhigh_ref, d_ref, near_ref, wt_ref, wl_ref)
    v = finish(scal_ref, w, below_ref, above_ref, 0, uin_ref, bin_ref, kx_ref, rows_ref)
    v_ref[...] = v - guess_ref[...]


def last_kernel(scal_ref, q_ref, rlow_ref, rhigh_ref, d_ref, near_ref, wt_ref, wl_ref,
                below_ref, above_ref, bin_ref, uin_ref, kx_ref, guess_ref, back0_ref, back1_ref, v1_ref, v2_ref, *refs):
    ends, (out_ref, rows_ref) = refs[:-2], refs[-2:]
    w = (q_ref, rlow_ref, rhigh_ref, d_ref, near_ref, wt_ref, wl_ref)
    v = finish(scal_ref, w, below_ref, above_ref, 0, uin_ref, bin_ref, kx_ref, rows_ref)
    out_ref[0] = reorder(v1_ref[...], back0_ref, back1_ref)
    out_ref[1] = reorder(v2_ref[...], back0_ref, back1_ref)
    out_ref[2] = reorder(v, back0_ref, back1_ref)
    turn = scal_ref[3]
    after = jnp.zeros((DOFS, ELEMS), F32)
    for k, end_ref in enumerate(ends):
        after = jnp.where(turn == k, end_ref[...], after)
    out_ref[3] = reorder(guess_ref[...] + after, back0_ref, back1_ref)


def start_kernel(q_ref, rlow_ref, rhigh_ref, d_ref, near_ref, wt_ref, wl_ref, v_ref, *outs):
    v = v_ref[...]
    begin((q_ref, rlow_ref, rhigh_ref, d_ref, near_ref, wt_ref, wl_ref), v, v, outs[:4], outs[4])


def turn_kernel(turn, first, more, scal_ref, q_ref, rlow_ref, rhigh_ref, d_ref, near_ref, wt_ref, wl_ref,
                below_ref, above_ref, bin_ref, uin_ref, kx_ref, res_ref, *outs):
    w = (q_ref, rlow_ref, rhigh_ref, d_ref, near_ref, wt_ref, wl_ref)
    v = finish(scal_ref, w, below_ref, above_ref, first, uin_ref, bin_ref, kx_ref, outs[-1])
    v = v + res_ref[scal_ref[5 + turn]]
    if more:
        begin(w, v, v, outs[:4], outs[4])
    else:
        outs[0][...] = v


STATE = ((DOFS, ELEMS), F32)
EDGE = ((2 * TRACE, LANES), F32)
FACES = ((TRACE // 2 * TRACE, LANES), F32)
EDGES = ((TRACE * DOFS, LANES), F32)
INVERSE = ((DOFS, DOFS, ELEMS), F32)
ROWS = pltpu.VMEM((DOFS, ELEMS), F32)
FACE_ROWS = pltpu.VMEM((TRACE, ELEMS), F32)
BEGUN = (STATE, STATE, EDGE, EDGE)
VMEM_LIMIT = 4 << 20


def near_by(x):
    return pltpu.with_memory_space_constraint(x, pltpu.VMEM)


def far_off(x):
    return pltpu.with_memory_space_constraint(x, pltpu.HBM)


def call(kernel, outs, scratch, *args, scalars=True, hbm_in=(), hbm_out=(), windows=(), limit=VMEM_LIMIT, busy=None):
    specs = [VMEM] * len(args)
    if scalars:
        specs[0] = SMEM
    for n in hbm_in:
        specs[n] = ANY
    return pl.pallas_call(
        kernel,
        out_shape=[(pltpu.HBM if n in (*hbm_out, *windows) else pltpu.VMEM)(*x) for n, x in enumerate(outs)],
        in_specs=specs,
        out_specs=[ANY if n in hbm_out else VMEM for n in range(len(outs))],
        scratch_shapes=scratch,
        compiler_params=pltpu.CompilerParams(vmem_limit_bytes=limit),
        cost_estimate=None if busy is None else pl.CostEstimate(flops=0, bytes_accessed=busy, transcendentals=0),
    )(*args)


class Operator:
    def __init__(self, inverse, rest, stream):
        self.inverse, self.rest, self.stream = inverse, rest, stream

    def call(self, kernel, outs, *args, scal=None, final=False, far=()):
        lead = [] if scal is None else [scal]
        fixed = [self.inverse, *self.rest]
        place, stream = len(lead), self.stream
        args = lead + fixed + list(args)
        specs = [SMEM] * place + [VMEM] * (len(args) - place)
        for n in range(place, len(args)):
            if n == place and stream:
                args[n] = far_off(args[n])
                specs[n] = ANY
            elif n - place - len(fixed) not in far:
                args[n] = near_by(args[n])

        def body(*refs):
            refs = list(refs)
            if stream:
                refs, (target, sems) = refs[:-2], refs[-2:]
                refs[place] = Stream(refs[place], target, sems)
            kernel(*refs)

        kind = jax.ShapeDtypeStruct if final else pltpu.VMEM
        fetch = [pltpu.VMEM((DOFS, DOFS, ELEMS), F32), pltpu.SemaphoreType.DMA((PARTS,))] if stream else []
        return pl.pallas_call(
            body,
            out_shape=[kind(*x) for x in outs],
            in_specs=specs,
            out_specs=[VMEM] * len(outs),
            scratch_shapes=[ROWS] + fetch,
            compiler_params=pltpu.CompilerParams(vmem_limit_bytes=(8 << 20) if stream else VMEM_LIMIT),
        )(*args)


def local(
    initial,
    guess,
    forcing,
    fine_inverse,
    coarse_inverse,
    neighbour,
    send_low,
    send_high,
    trace_map,
    lift_map,
):
    times = lax.axis_size("tm")
    blocks = lax.axis_size("space")
    now = lax.axis_index("tm")
    place = lax.axis_index("space")
    guess = guess[0]

    def route(target):
        return [
            (t * blocks + s, a * blocks + b)
            for t in range(times)
            for s in range(blocks)
            for a, b in [target(t, s)]
        ]

    def shift(by, flip=0):
        def target(t, s):
            there = s + by
            t = t ^ flip
            return (t if 0 <= there < blocks else t ^ HALF), there % blocks

        return route(target)

    up, down = shift(1), shift(-1)
    chain_up, chain_down = shift(1, 1), shift(-1, 1)
    swap_cores = route(lambda t, s: (t ^ 1, s))
    swap_halves = route(lambda t, s: (t ^ HALF, s))

    def move(x, pairs):
        return lax.ppermute(x, ("tm", "space"), pairs)

    def exchange(low, high, up=up, down=down):
        above = move(low, down)
        below = move(high, up)
        return below, above

    group, core = now % HALF // 2, now % 2
    turns = jnp.arange(HALF)
    slots = (group - turns // 2) % 4 + 4 * (turns % 2 ^ core)
    early = now < HALF
    turn = now % HALF
    before = jnp.where(early, turn - 1, HALF + turn)
    after = jnp.where(early, turn, HALF + turn + 1)
    scal = jnp.concatenate([jnp.stack([place > 0, place < blocks - 1, before, after, core]), slots]).astype(jnp.int32)

    slow, shigh = send_low.reshape(1, LANES), send_high.reshape(1, LANES)
    traces = trace_map.reshape(6 * TRACE, DOFS)
    lifts = jnp.transpose(lift_map, (0, 2, 1)).reshape(6 * TRACE, DOFS)
    ahead = [(i, i + 1) for i in range(times - 1)]
    moved = lax.ppermute(guess, "tm", ahead)

    def prepare(inverse, scal, windows=()):
        q, d, rlow, rhigh, klow, khigh = call(
            prepare_kernel,
            [INVERSE, STATE, EDGES, EDGES, FACES, FACES],
            [pltpu.VMEM((DOFS, DOFS, ELEMS), F32)] + [pltpu.SemaphoreType.DMA((DOFS // 8,))] * 2,
            scal, *map(far_off, (inverse, slow, shigh, traces, lifts)),
            hbm_in=(1,), hbm_out=(0,), windows=windows, limit=10 << 20, busy=24 << 20,
        )
        return q, (rlow, rhigh, d), (klow, khigh)

    def both_halves(faces):
        return (*faces, *[move(x, swap_cores) for x in faces])

    def cross(faces, low, high):
        args = [near_by(x) for x in (*faces, low, high)]
        (kx,) = call(cross_kernel, [EDGE], [FACE_ROWS], scal, *args, busy=2 << 20)
        return kx

    fine_inverse, fine_rest, fine_faces = prepare(fine_inverse, scal)
    fine_faces = exchange(*fine_faces)
    wt, wl, near, back0, back1 = call(
        tables_kernel,
        [((192, 192), BF16), ((64, 576), BF16), ((16, LANES), jnp.int32), ((1, LANES), jnp.int32), ((1, LANES), jnp.int32)],
        [],
        *map(far_off, (traces, jnp.transpose(lift_map, (1, 0, 2)).reshape(DOFS, 6 * TRACE), neighbour, slow, shigh)),
        scalars=False,
    )
    forces, goal = call(
        reorder_kernel, [((4, DOFS, ELEMS), F32), STATE], [], *map(far_off, (forcing, guess, slow, shigh)), scalars=False
    )
    fine = Operator(fine_inverse, (*fine_rest, near, wt, wl), False)
    start = jnp.where(now == 0, initial, moved)
    anchor, b, u, low, high = fine.call(
        first_kernel, [STATE, *BEGUN], start, far_off(slow), far_off(shigh), forces, far=(0, 1, 2)
    )
    low, high, later = lax.optimization_barrier((low, high, scal))
    coarse_inverse, coarse_rest, coarse_faces = prepare(coarse_inverse, later, (2, 3, 4, 5))
    fine_faces = both_halves(lax.optimization_barrier((*fine_faces, coarse_rest[2]))[:2])

    def fine_step(step, keep, b, u, low, high):
        kx = cross(fine_faces, low, high)
        below, above = exchange(low, high)
        return fine.call(
            functools.partial(fine_kernel, step, keep), [*BEGUN, STATE] if keep else BEGUN,
            below, above, b, u, kx, forces, scal=scal,
        )

    for step in (1, 2, 3):
        b, u, low, high = fine_step(step, False, b, u, low, high)
    kx = cross(fine_faces, low, high)
    below, above = exchange(low, high)
    fetched = Operator(fine_inverse, fine.rest, True)
    (residual,) = fetched.call(residual_kernel, [STATE], below, above, b, u, kx, goal, scal=scal)

    residual, coarse_inverse, coarse_rest, coarse_faces = lax.optimization_barrier(
        (residual, coarse_inverse, coarse_rest, coarse_faces)
    )
    coarse = Operator(coarse_inverse, (*coarse_rest, near, wt, wl), False)
    coarse_faces = both_halves(exchange(*coarse_faces))

    def turned(k):
        return route(lambda t, s: (t // HALF * HALF + (t % HALF + 2 * k) % HALF, s))

    held = jnp.stack([residual] + [move(residual, turned(k)) for k in (1, 2, 3)])
    held = jnp.concatenate([held, move(held, swap_cores)])

    def chain(first, count, b, u, low, high, edges=None):
        ends = []
        for turn in range(first, first + count):
            kx = cross(coarse_faces, low, high)
            below, above = exchange(low, high, chain_up, chain_down) if edges is None else edges
            edges = None
            b, u, low, high = coarse.call(
                functools.partial(turn_kernel, turn, 0, True), BEGUN, below, above, b, u, kx, held, scal=scal
            )
            ends.append(b)
        return ends, (b, u, low, high)

    base = lax.dynamic_index_in_dim(held, scal[5], 0, False)
    early_ends, (b, u, low, high) = chain(1, HALF - 1, *coarse.call(start_kernel, BEGUN, base))
    early_ends = [base] + early_ends
    edges = exchange(low, high, shift(1, HALF + 1), shift(-1, HALF + 1))
    late_start = move(b, swap_halves)
    late_ends, (cb, cu, clow, chigh) = chain(0, HALF - 1, *coarse.call(start_kernel, BEGUN, late_start), edges)
    late_ends = [late_start] + late_ends

    b, u, low, high = fine.call(again_kernel, BEGUN, anchor, forces, *early_ends, *late_ends, scal=scal)
    ckx = cross(coarse_faces, clow, chigh)
    kx = cross(fine_faces, low, high)
    both = lax.optimization_barrier((jnp.concatenate([low, clow]), jnp.concatenate([high, chigh])))
    below, above = exchange(*both)
    b, u, low, high, v1 = fine.call(
        functools.partial(fine_kernel, 1, True), [*BEGUN, STATE], below, above, b, u, kx, forces, scal=scal
    )
    (last_end,) = coarse.call(
        functools.partial(turn_kernel, HALF - 1, 2 * TRACE, False), [STATE], below, above, cb, cu, ckx, held, scal=scal
    )
    b, u, low, high, v2 = fine_step(2, True, b, u, low, high)
    kx = cross(fine_faces, low, high)
    below, above = exchange(low, high)
    (out,) = fine.call(
        last_kernel, [((4, DOFS, ELEMS), F32)],
        below, above, b, u, kx, goal, back0, back1, v1, v2, *early_ends, *late_ends, last_end,
        scal=scal, final=True,
    )
    return out


def solution(mesh):
    in_specs = (
        P(None, "space"),
        P("tm", None, "space"),
        P("tm", None, "space"),
        P(None, None, "space"),
        P(None, None, "space"),
        P(None, "space"),
        P("space"),
        P("space"),
        P(),
        P(),
    )
    out_specs = P("tm", None, "space")
    return jax.shard_map(local, mesh=mesh, in_specs=in_specs, out_specs=out_specs, check_vma=False)
```
